32 devices in a mesh: leaf: 8 (over z, y), samp: 4 (over x, core).
Axes of the slice: x: 2, y: 2, z: 4, core: 2. Of those that a mesh axis runs over, the one named last changes fastest.
Arguments:
- samples: bfloat16 [32768, 256], P('leaf', 'samp'), may hold values from -6 to 6
- omega: bfloat16 [32768, 256], P('leaf', 'samp'), may hold values from -6 to 6
- leaf_basis: bfloat16 [256, 64, 128], P('leaf'), may hold values from -0.5 to 0.5
- near_blocks: bfloat16 [256, 8, 128, 128], P('leaf'), may hold values from -0.1875 to 0.1875
- near_index: int32 [256, 8], P('leaf'), may hold values from 0 to 255, as said below
- near_count: int32 [256], P('leaf'), may hold values from 2 to 8, as said below
- inner_transfer: bfloat16 [496, 4096], P('leaf'), may hold values from -0.5 to 0.5
- upper_transfer: bfloat16 [14, 4096], replicated, may hold values from -0.5 to 0.5
Outputs:
- leaf_coeffs: float32 [256, 64, 256], P('leaf', None, 'samp')
- leaf_gram: float32 [256, 4096], P('leaf', 'samp')
- ancestor_coeffs: float32 [8, 3, 64, 256], P('leaf', None, None, 'samp')
The draws below stay inside these ranges and needn't reach their ends.
Inputs may be any that keep to these rules, and one draw needn't show every extreme that they name: `near_index`: slot 0 of leaf i names i itself, slot 1 names a leaf exactly 32 away from i, and every slot names a leaf at most 32 away from i. `near_count`: every group of 32 consecutive leaves has a leaf with all 8 slots live.
All inputs are finite; a program needn't handle non-finite values.
Results may differ from the reference program's by a relative error of at most 0.0029.
Values may be sent and summed in bfloat16 or wider, within the bound.
A program may use at most 64 MiB of HBM per device.

```python
import jax
import jax.numpy as jnp
from jax import lax

LEAF = 128
R = 64
NB = 8
LEAF_DEV = 32
LEAVES = 256
POINTS = 32768
SAMPLE_COLUMNS = 256
INNER_NODES = 496
UPPER_TREE_NODES = 14
N_LEAF = 8


def draw_near_index(key, part):
    key_offset = jax.random.fold_in(key, 11)
    key_sign = jax.random.fold_in(key, 12)
    offsets = jax.random.randint(key_offset, (LEAVES, NB), -LEAF_DEV, LEAF_DEV + 1)
    sign_draw = 2 * jax.random.randint(key_sign, (LEAVES, 1), 0, 2) - 1
    column = jnp.arange(NB)[None, :]
    offsets = jnp.where(column == 0, 0, jnp.where(column == 1, sign_draw * LEAF_DEV, offsets))
    self_leaf_block = jnp.arange(LEAVES)[:, None]
    target = self_leaf_block + offsets
    inside = (target >= 0) & (target < LEAVES)
    return jnp.where(inside, target, self_leaf_block - offsets).astype(jnp.int32)


def draw_near_count(key, part):
    key_count = jax.random.fold_in(key, 21)
    key_place = jax.random.fold_in(key, 22)
    counts = jax.random.randint(key_count, (LEAVES,), 2, NB + 1)
    selected_entries = jax.random.randint(key_place, (), 0, LEAF_DEV)
    position = jnp.arange(LEAVES) % LEAF_DEV
    return jnp.where(position == selected_entries, NB, counts).astype(jnp.int32)


def level_of(key, dims, cuts, smallest, high):
    gain = 1.0
    for dim, parts in cuts:
        draws = jax.random.uniform(jax.random.fold_in(jax.random.fold_in(key, 6), dim), (parts,), jnp.float32, smallest / len(cuts), high / len(cuts))
        gain = gain * jnp.repeat(jnp.exp(draws), dims[dim] // parts).reshape((-1,) + (1,) * (len(dims) - 1 - dim))
    return gain


def gaussian(own_key, shape, width, reach, shards=(), kind=jnp.bfloat16):
    array = width * jax.random.normal(own_key, shape, jnp.float32)
    if shards:
        array = array * level_of(own_key, shape, shards, -0.22, 0.18)
    return jnp.clip(array, -reach, reach).astype(kind)


def setup_inputs(seed: int = 0) -> dict:
    key_list = jax.random.split(jax.random.key(seed), 9)
    samples = gaussian(key_list[0], (POINTS, SAMPLE_COLUMNS), 1.0, 6.0, ((0, 8), (1, 4)))
    omega = gaussian(key_list[1], (POINTS, SAMPLE_COLUMNS), 1.0, 6.0, ((0, 8), (1, 4)))
    leaf_basis = gaussian(key_list[2], (LEAVES, R, LEAF), LEAF ** -0.5, 0.5, ((0, 8),))
    near_blocks = gaussian(key_list[3], (LEAVES, NB, LEAF, LEAF), (LEAF * NB) ** -0.5, 0.1875, ((0, 8),))
    near_index = draw_near_index(jax.random.fold_in(key_list[8], 71), 0)
    near_count = draw_near_count(jax.random.fold_in(key_list[8], 71), 0)
    inner_transfer = gaussian(key_list[6], (INNER_NODES, R * R), (2 * R) ** -0.5, 0.5, ((0, 8),))
    upper_transfer = gaussian(key_list[7], (UPPER_TREE_NODES, R * R), (2 * R) ** -0.5, 0.5)
    return {"samples": samples, "omega": omega, "leaf_basis": leaf_basis, "near_blocks": near_blocks, "near_index": near_index, "near_count": near_count, "inner_transfer": inner_transfer, "upper_transfer": upper_transfer}


def merge_levels(current, transfer, node_count):
    offset = 0
    width_now = node_count
    while width_now > 1:
        mats = transfer[:, offset:offset + width_now]
        projected = jnp.einsum('gnab,gnas->gnbs', mats, current, precision=lax.Precision.HIGHEST)
        shape_now = projected.shape
        projected = projected.reshape(shape_now[0], width_now // 2, 2, shape_now[2], shape_now[3])
        current = projected[:, :, 0] + projected[:, :, 1]
        offset = offset + width_now
        width_now = width_now // 2
    return current[:, 0]


def upper_levels(current, transfer, node_count):
    offset = 0
    width_now = node_count
    levels = []
    while width_now > 1:
        mats = transfer[offset:offset + width_now]
        projected = jnp.einsum('nab,nas->nbs', mats, current, precision=lax.Precision.HIGHEST)
        projected = projected.reshape(width_now // 2, 2, projected.shape[1], projected.shape[2])
        current = projected[:, 0] + projected[:, 1]
        levels.append(jnp.repeat(current, node_count // (width_now // 2), axis=0))
        offset = offset + width_now
        width_now = width_now // 2
    return jnp.stack(levels, axis=1)


def reference(samples, omega, leaf_basis, near_blocks, near_index, near_count, inner_transfer, upper_transfer):
    omega_leaves = omega.reshape(LEAVES, LEAF, SAMPLE_COLUMNS)
    slot_identifiers = jnp.arange(NB)

    def leaf_group(inputs):
        blocks, index_rows, count_rows, sample_rows, basis = inputs
        fetched = omega_leaves[index_rows].astype(jnp.float32)
        live_mask = (slot_identifiers[None, :] < count_rows[:, None]).astype(jnp.float32)
        near_sum = jnp.einsum('gkab,gkbs,gk->gas', blocks.astype(jnp.float32), fetched, live_mask)
        far_part = (sample_rows.astype(jnp.float32) - near_sum).astype(jnp.bfloat16)
        return jnp.einsum('grb,gbs->grs', basis.astype(jnp.float32), far_part.astype(jnp.float32))

    cluster_coefficient_array = lax.map(leaf_group, (
        near_blocks.reshape(N_LEAF, LEAF_DEV, NB, LEAF, LEAF),
        near_index.reshape(N_LEAF, LEAF_DEV, NB),
        near_count.reshape(N_LEAF, LEAF_DEV),
        samples.reshape(N_LEAF, LEAF_DEV, LEAF, SAMPLE_COLUMNS),
        leaf_basis.reshape(N_LEAF, LEAF_DEV, R, LEAF)))
    leaf_coeffs = cluster_coefficient_array.reshape(LEAVES, R, SAMPLE_COLUMNS)
    gram = jnp.einsum('lrs,lts->lrt', leaf_coeffs, leaf_coeffs, precision=lax.Precision.HIGHEST) / SAMPLE_COLUMNS
    leaf_gram = gram.reshape(LEAVES, R * R)
    inner = inner_transfer.astype(jnp.float32).reshape(N_LEAF, 2 * LEAF_DEV - 2, R, R)
    group_coeffs = merge_levels(cluster_coefficient_array, inner, LEAF_DEV)
    upper = upper_transfer.astype(jnp.float32).reshape(UPPER_TREE_NODES, R, R)
    ancestor_coeffs = upper_levels(group_coeffs, upper, N_LEAF)
    return leaf_coeffs, leaf_gram, ancestor_coeffs
```

```python
import functools

import jax
import jax.numpy as jnp
from jax import lax
from jax.experimental import pallas as pl
from jax.experimental.pallas import tpu as pltpu
from jax.sharding import PartitionSpec as P

MESH = pl.DeviceIdType.MESH
F32 = jnp.float32
BF16 = jnp.bfloat16


def split(x):
    high = x.astype(BF16)
    return high, (x - high.astype(F32)).astype(BF16)


def dot_nt(a, b):
    return lax.dot_general(a, b, (((1,), (1,)), ((), ())), preferred_element_type=F32)


def dot(a, b):
    return jnp.dot(a, b, preferred_element_type=F32)


def chain_step(rows, mats):
    high, low = split(rows)
    n = rows.shape[0]
    both = dot_nt(jnp.concatenate([high, low], axis=0), mats)
    return both[:n] + both[n:]


def kernel(
    n_leaf, n_samp, total_columns,
    index_ref, count_ref, inner_ref, upper_ref, omega_hbm, samples_hbm, basis_hbm, near_hbm,
    coeff_hbm, gram_ref, ancestor_ref,
    omega_v, samples_v, basis_v, near_v, own, land_l, land_r, held, packed,
    inner_v, upper_v, paths, leaf_high, leaf_low, up_acc, up_send, up_recv,
    gram_send, gram_recv, gram_sum, gram_mix, coeff_v,
    load_sem, near_sem, send_l, send_r, recv_l, recv_r,
    gram_ssem, gram_rsem, up_ssem, up_rsem, out_sem,
):
    leaf = lax.axis_index("leaf")
    samp = lax.axis_index("samp")
    leaf_count, rank, leaf_size = basis_v.shape
    slots = near_v.shape[1]
    width = omega_v.shape[0]
    pairs = leaf_count // 2
    half = pairs // 2
    heights = ancestor_ref.shape[0]
    chunk = 2
    steps = half // chunk
    part = rank // n_samp
    nodes = inner_ref.shape[0]

    load_omega = pltpu.make_async_copy(omega_hbm, omega_v, load_sem.at[0])
    load_samples = pltpu.make_async_copy(samples_hbm, samples_v, load_sem.at[1])
    load_basis = pltpu.make_async_copy(basis_hbm, basis_v, load_sem.at[2])
    load_near = pltpu.make_async_copy(near_hbm, near_v, near_sem)
    load_omega.start()
    load_samples.start()
    load_basis.start()
    load_near.start()

    barrier = pltpu.get_barrier_semaphore()
    for d in range(1, n_leaf):
        pl.semaphore_signal(barrier, inc=1, device_id=(leaf ^ d, samp), device_id_type=MESH)
    for d in range(1, n_samp):
        pl.semaphore_signal(barrier, inc=1, device_id=(leaf, samp ^ d), device_id_type=MESH)

    load_omega.wait()

    def pair_tile(src, u):
        at = pl.multiple_of(u * 2 * leaf_size, 2 * leaf_size)
        rows = jnp.concatenate(
            [src[:, pl.ds(at, leaf_size)], src[:, pl.ds(at + leaf_size, leaf_size)]], axis=0
        )
        return rows.T

    def pack_omega(u, carry):
        tile = pair_tile(omega_v, u)
        own[u] = tile
        held[pairs + u] = tile
        return carry

    lax.fori_loop(0, pairs, pack_omega, 0)
    pl.semaphore_wait(barrier, n_leaf + n_samp - 2)

    def to_right(c):
        lo, size = (half, half) if c == 0 else (half - chunk * c, chunk)
        return pltpu.make_async_remote_copy(
            src_ref=own.at[pl.ds(lo, size)], dst_ref=land_l.at[pl.ds(lo, size)],
            send_sem=send_r.at[c], recv_sem=recv_l.at[c],
            device_id=(leaf + 1, samp), device_id_type=MESH,
        )

    def to_left(c):
        lo, size = (0, half) if c == 0 else (half + chunk * (c - 1), chunk)
        return pltpu.make_async_remote_copy(
            src_ref=own.at[pl.ds(lo, size)], dst_ref=land_r.at[pl.ds(lo, size)],
            send_sem=send_l.at[c], recv_sem=recv_r.at[c],
            device_id=(leaf - 1, samp), device_id_type=MESH,
        )

    for c in range(steps + 1):
        @pl.when(leaf < n_leaf - 1)
        def _():
            to_right(c).start()

        @pl.when(leaf > 0)
        def _():
            to_left(c).start()

    for r in range(rank * rank // 128):
        for src, dst in ((inner_ref, inner_v), (upper_ref, upper_v)):
            count = src.shape[0]
            tile = src[:, 128 * r:128 * r + 128].astype(F32)
            dst[pl.ds(2 * r, count, stride=rank), :] = tile
            dst[pl.ds(2 * r + 1, count, stride=rank), :] = pltpu.roll(tile, 64, 1)

    eye = (
        lax.broadcasted_iota(jnp.int32, (rank, rank), 0)
        == lax.broadcasted_iota(jnp.int32, (rank, rank), 1)
    ).astype(F32)
    rows = None
    starts = []
    offset = 0
    for h in range(heights):
        starts.append(offset)
        offset += n_leaf >> h
    for h in reversed(range(heights)):
        node = starts[h] + lax.shift_right_logical(leaf, h)
        mat = upper_v[pl.ds(pl.multiple_of(node * rank, rank), rank), :][:, :rank].astype(BF16)
        rows = eye if rows is None else jnp.concatenate([eye, rows], axis=0)
        rows = chain_step(rows, mat)
    paths[nodes] = rows

    def children(q):
        mats = inner_v[pl.ds(pl.multiple_of(q * 2 * rank, 2 * rank), 2 * rank), :]
        return chain_step(paths[leaf_count + q], mats[:, :rank].astype(BF16))

    def inner_pair(i, carry):
        q = leaf_count - 2 - i
        both = children(q)
        paths[2 * q] = both[:, :rank]
        paths[2 * q + 1] = pltpu.roll(both, 64, 1)[:, :rank]
        return carry

    lax.fori_loop(0, pairs - 1, inner_pair, 0)

    def leaf_pair(q, carry):
        high, low = split(children(q))
        leaf_high[q] = high
        leaf_low[q] = low
        return carry

    lax.fori_loop(0, pairs, leaf_pair, 0)

    load_samples.wait()

    def pack_samples(u, carry):
        packed[u] = pair_tile(samples_v, u)
        return carry

    lax.fori_loop(0, pairs, pack_samples, 0)
    up_acc[...] = jnp.zeros_like(up_acc)
    load_basis.wait()
    load_near.wait()

    lane_half = lax.broadcasted_iota(jnp.int32, (1, 128), 1) // 64
    lower = lax.broadcasted_iota(jnp.int32, (leaf_size, 128), 1) < 64
    base = leaf * leaf_count - leaf_count

    def near_product(p):
        tiles = []
        for k in range(slots):
            at = jnp.clip(index_ref[k, p] - base, 0, 3 * leaf_count - 1)
            want = jnp.where(k < count_ref[p], at % 2, 2)
            mask = (lane_half == want).astype(F32).astype(BF16)
            tiles.append(held[at // 2] * mask)
        left = jnp.concatenate([near_v[p, k] for k in range(slots)], axis=1)
        total = dot(left, jnp.concatenate(tiles, axis=0))
        return total + pltpu.roll(total, 64, 1)

    def process(u, w):
        near = jnp.where(lower, near_product(2 * u), near_product(2 * u + 1))
        far = (packed[u].astype(F32) - near).astype(BF16)
        basis = basis_v[pl.ds(2 * u, 2)].reshape(2 * rank, leaf_size)
        both = dot(basis, far)
        top, bottom = both[:rank], both[rank:]
        coeff_v[2 * u] = top[:, :width]
        coeff_v[2 * u + 1] = pltpu.roll(bottom, 64, 1)[:, :width]
        low_lane = lower[:rank]
        top = jnp.where(low_lane, top, 0.0)
        bottom = jnp.where(low_lane, 0.0, bottom)
        top_high, top_low = split(top)
        bottom_high, bottom_low = split(bottom)
        block_high = jnp.concatenate([top_high, bottom_high], axis=0)
        block_low = jnp.concatenate([top_low, bottom_low], axis=0)
        row_high = top_high + bottom_high
        row_low = top_low + bottom_low
        gram = dot_nt(
            jnp.concatenate([row_high, row_high, row_low], axis=1),
            jnp.concatenate([block_high, block_low, block_high], axis=1),
        ) * (1.0 / total_columns)
        for t in range(n_samp):
            gram_send[t, pl.ds(pl.multiple_of(w * part, part), part), :] = (
                gram[t * part:(t + 1) * part].astype(gram_send.dtype)
            )
        path_high, path_low = leaf_high[u], leaf_low[u]
        up_acc[...] += dot(
            jnp.concatenate([path_high, path_high, path_low], axis=1),
            jnp.concatenate([block_high, block_low, block_high], axis=0),
        )

    def accept(land, at_held, lo, size):
        def body(i, carry):
            held[at_held + lo + i] = land[lo + i]
            return carry

        lax.fori_loop(0, size, body, 0)

    @pl.when(leaf > 0)
    def _():
        to_right(0).wait_recv()
        accept(land_l, 0, half, half)

    @pl.when(leaf < n_leaf - 1)
    def _():
        to_left(0).wait_recv()
        accept(land_r, 2 * pairs, 0, half)

    span = 2 * chunk * part

    def gram_copy(d, j):
        at = pl.ds(pl.multiple_of(j * span, span), span)
        return pltpu.make_async_remote_copy(
            src_ref=gram_send.at[samp ^ d, at], dst_ref=gram_recv.at[d - 1, at],
            send_sem=gram_ssem.at[d - 1, j], recv_sem=gram_rsem.at[d - 1, j],
            device_id=(leaf, samp ^ d), device_id_type=MESH,
        )

    def out_copy(j, side):
        lo = 2 * (half - chunk * (j + 1)) if side == 0 else 2 * (half + chunk * j)
        at = pl.ds(lo, 2 * chunk)
        return pltpu.make_async_copy(coeff_v.at[at], coeff_hbm.at[at], out_sem.at[side, j])

    for j in range(steps):
        lo_l = half - chunk * (j + 1)
        lo_r = half + chunk * j

        @pl.when(leaf > 0)
        def _():
            to_right(j + 1).wait_recv()
            accept(land_l, 0, lo_l, chunk)

        @pl.when(leaf < n_leaf - 1)
        def _():
            to_left(j + 1).wait_recv()
            accept(land_r, 2 * pairs, lo_r, chunk)

        def body(i, carry):
            process(lo_l + i, 2 * chunk * j + i)
            process(lo_r + i, 2 * chunk * j + chunk + i)
            return carry

        lax.fori_loop(0, chunk, body, 0)
        for d in range(1, n_samp):
            gram_copy(d, j).start()
        out_copy(j, 0).start()
        out_copy(j, 1).start()

    total = up_acc[...]
    total = total + pltpu.roll(total, 64, 1)
    side = rank // 2
    for h in range(heights):
        up_send[h * side:(h + 1) * side] = jnp.where(
            lower[:side], total[h * rank:h * rank + side], total[h * rank + side:(h + 1) * rank]
        )

    def up_copy(d):
        first = (d.bit_length() - 1) * side
        at = pl.ds(first, heights * side - first)
        return pltpu.make_async_remote_copy(
            src_ref=up_send.at[at], dst_ref=up_recv.at[d - 1, at],
            send_sem=up_ssem.at[d - 1], recv_sem=up_rsem.at[d - 1],
            device_id=(leaf ^ d, samp), device_id_type=MESH,
        )

    for d in range(1, n_leaf):
        up_copy(d).start()

    for j in range(steps):
        for d in range(1, n_samp):
            gram_copy(d, j).wait_recv()
    for w in range(pairs):
        j, i = divmod(w, 2 * chunk)
        u = half - chunk * (j + 1) + i if i < chunk else half + chunk * j + i - chunk
        at = slice(w * part, (w + 1) * part)
        value = gram_send[samp, at, :].astype(F32)
        for d in range(1, n_samp):
            value = value + gram_recv[d - 1, at, :].astype(F32)
        gram_sum[u * part:(u + 1) * part, :] = value
    low16 = lower[:pairs]
    for m in range(part // 2):
        first = gram_sum[pl.ds(2 * m, pairs, stride=part), :]
        second = gram_sum[pl.ds(2 * m + 1, pairs, stride=part), :]
        even = jnp.where(low16, first, pltpu.roll(second, 64, 1))
        odd = jnp.where(low16, pltpu.roll(first, 64, 1), second)
        lo = m * leaf_count
        gram_mix[pl.ds(lo, pairs, stride=2), :] = even
        gram_mix[pl.ds(lo + 1, pairs, stride=2), :] = odd
        gram_ref[:, 128 * m:128 * m + 128] = gram_mix[lo:lo + leaf_count, :]

    for d in range(1, n_leaf):
        up_copy(d).wait_recv()
    for h in range(heights):
        at = slice(h * side, (h + 1) * side)
        value = up_send[at, :]
        for d in range(1, n_leaf):
            if d.bit_length() <= h + 1:
                value = value + up_recv[d - 1, at, :]
        ancestor_ref[h, 0:side, :] = value[:, :width]
        ancestor_ref[h, side:rank, :] = pltpu.roll(value, 64, 1)[:, :width]

    for c in range(steps + 1):
        @pl.when(leaf < n_leaf - 1)
        def _():
            to_right(c).wait_send()

        @pl.when(leaf > 0)
        def _():
            to_left(c).wait_send()

    for j in range(steps):
        for d in range(1, n_samp):
            gram_copy(d, j).wait_send()
        out_copy(j, 0).wait()
        out_copy(j, 1).wait()
    for d in range(1, n_leaf):
        up_copy(d).wait_send()


def shards(
    n_leaf, n_samp,
    samples, omega, leaf_basis, near_blocks, near_index, near_count, inner_transfer, upper_transfer
):
    leaf_count, rank, leaf_size = leaf_basis.shape
    width = samples.shape[1]
    pairs = leaf_count // 2
    steps = pairs // 4
    heights = n_leaf.bit_length() - 1
    part = rank // n_samp
    nodes = inner_transfer.shape[0]
    upper_nodes = upper_transfer.shape[0]
    wire = BF16 if part % 16 == 0 else F32
    omega, samples, near_index = omega.T, samples.T, near_index.T
    vmem = pl.BlockSpec(memory_space=pltpu.VMEM)
    smem = pl.BlockSpec(memory_space=pltpu.SMEM)
    hbm = pl.BlockSpec(memory_space=pl.ANY)
    dma = pltpu.SemaphoreType.DMA
    coeffs, gram, ancestors = pl.pallas_call(
        functools.partial(kernel, n_leaf, n_samp, width * n_samp),
        out_shape=(
            jax.ShapeDtypeStruct((leaf_count, rank, width), F32),
            jax.ShapeDtypeStruct((leaf_count, part * rank), F32),
            jax.ShapeDtypeStruct((heights, rank, width), F32),
        ),
        in_specs=[smem, smem, vmem, vmem, hbm, hbm, hbm, hbm],
        out_specs=(hbm, vmem, vmem),
        scratch_shapes=[
            pltpu.VMEM(omega.shape, BF16),
            pltpu.VMEM(samples.shape, BF16),
            pltpu.VMEM(leaf_basis.shape, BF16),
            pltpu.VMEM(near_blocks.shape, BF16),
            pltpu.VMEM((pairs, leaf_size, 128), BF16),
            pltpu.VMEM((pairs, leaf_size, 128), BF16),
            pltpu.VMEM((pairs, leaf_size, 128), BF16),
            pltpu.VMEM((3 * pairs, leaf_size, 128), BF16),
            pltpu.VMEM((pairs, leaf_size, 128), BF16),
            pltpu.VMEM((nodes * rank, 128), F32),
            pltpu.VMEM((upper_nodes * rank, 128), F32),
            pltpu.VMEM((nodes + 1, heights * rank, rank), F32),
            pltpu.VMEM((pairs, heights * rank, 128), BF16),
            pltpu.VMEM((pairs, heights * rank, 128), BF16),
            pltpu.VMEM((heights * rank, 128), F32),
            pltpu.VMEM((heights * rank // 2, 128), F32),
            pltpu.VMEM((n_leaf - 1, heights * rank // 2, 128), F32),
            pltpu.VMEM((n_samp, pairs * part, 128), wire),
            pltpu.VMEM((n_samp - 1, pairs * part, 128), wire),
            pltpu.VMEM((pairs * part, 128), F32),
            pltpu.VMEM((part // 2 * leaf_count, 128), F32),
            pltpu.VMEM((leaf_count, rank, width), F32),
            dma((3,)), dma,
            dma((steps + 1,)), dma((steps + 1,)), dma((steps + 1,)), dma((steps + 1,)),
            dma((n_samp - 1, steps)), dma((n_samp - 1, steps)),
            dma((n_leaf - 1,)), dma((n_leaf - 1,)),
            dma((2, steps)),
        ],
        compiler_params=pltpu.CompilerParams(
            collective_id=0, has_side_effects=True, vmem_limit_bytes=56 * 1024 * 1024
        ),
    )(near_index, near_count, inner_transfer, upper_transfer, omega, samples, leaf_basis, near_blocks)
    return coeffs, gram, ancestors[None]


def solution(mesh):
    return jax.shard_map(
        functools.partial(shards, mesh.shape["leaf"], mesh.shape["samp"]),
        mesh=mesh,
        in_specs=(
            P("leaf", "samp"),
            P("leaf", "samp"),
            P("leaf", None, None),
            P("leaf", None, None, None),
            P("leaf", None),
            P("leaf"),
            P("leaf", None),
            P(),
        ),
        out_specs=(P("leaf", None, "samp"), P("leaf", "samp"), P("leaf", None, None, "samp")),
        check_vma=False,
    )
```

```python
import functools

import jax
import jax.numpy as jnp
from jax import lax
from jax.experimental import pallas as pl
from jax.experimental.pallas import tpu as pltpu
from jax.sharding import PartitionSpec as P

MESH = pl.DeviceIdType.MESH
F32 = jnp.float32
BF16 = jnp.bfloat16


def split(x):
    high = x.astype(BF16)
    return high, (x - high.astype(F32)).astype(BF16)


def dot_nt(a, b):
    return lax.dot_general(a, b, (((1,), (1,)), ((), ())), preferred_element_type=F32)


def dot(a, b):
    return jnp.dot(a, b, preferred_element_type=F32)


def chain_step(rows, mats):
    high, low = split(rows)
    n = rows.shape[0]
    both = dot_nt(jnp.concatenate([high, low], axis=0), mats)
    return both[:n] + both[n:]


def kernel(
    n_leaf, n_samp, total_columns,
    index_ref, count_ref, inner_ref, upper_ref, omega_hbm, samples_hbm, basis_hbm, near_hbm,
    coeff_hbm, gram_ref, ancestor_ref,
    omega_v, samples_v, basis_v, near_v, own, land_l, land_r, held, packed,
    inner_v, upper_v, paths, ascend, leaf_path, up_acc, up_send, up_recv,
    gram_send, gram_recv, gram_sum, gram_mix, coeff_v,
    load_sem, near_sem, send_l, send_r, recv_l, recv_r,
    gram_ssem, gram_rsem, up_ssem, up_rsem, out_sem,
):
    leaf = lax.axis_index("leaf")
    samp = lax.axis_index("samp")
    leaf_count, rank, leaf_size = basis_v.shape
    slots = near_v.shape[1]
    width = omega_v.shape[0]
    pairs = leaf_count // 2
    half = pairs // 2
    heights = ancestor_ref.shape[0]
    steps = half
    part = rank // n_samp
    nodes = inner_ref.shape[0]

    load_omega = pltpu.make_async_copy(omega_hbm, omega_v, load_sem.at[0])
    load_samples = pltpu.make_async_copy(samples_hbm, samples_v, load_sem.at[1])
    load_basis = pltpu.make_async_copy(basis_hbm, basis_v, load_sem.at[2])
    load_near = pltpu.make_async_copy(near_hbm, near_v, near_sem)
    load_omega.start()
    load_samples.start()
    load_basis.start()
    load_near.start()

    barrier = pltpu.get_barrier_semaphore()
    for d in range(1, n_leaf):
        pl.semaphore_signal(barrier, inc=1, device_id=(leaf ^ d, samp), device_id_type=MESH)
    for d in range(1, n_samp):
        pl.semaphore_signal(barrier, inc=1, device_id=(leaf, samp ^ d), device_id_type=MESH)

    load_omega.wait()

    def pair_tile(src, u):
        at = pl.multiple_of(u * 2 * leaf_size, 2 * leaf_size)
        rows = jnp.concatenate(
            [src[:, pl.ds(at, leaf_size)], src[:, pl.ds(at + leaf_size, leaf_size)]], axis=0
        )
        return rows.T

    def pack_omega(u, carry):
        tile = pair_tile(omega_v, u)
        own[u] = tile
        held[pairs + u] = tile
        return carry

    lax.fori_loop(0, pairs, pack_omega, 0, unroll=4)
    pl.semaphore_wait(barrier, n_leaf + n_samp - 2)

    def to_right(c, lo, size=1):
        return pltpu.make_async_remote_copy(
            src_ref=own.at[pl.ds(lo, size)], dst_ref=land_l.at[pl.ds(lo, size)],
            send_sem=send_r.at[c], recv_sem=recv_l.at[c],
            device_id=(leaf + 1, samp), device_id_type=MESH,
        )

    def to_left(c, lo, size=1):
        return pltpu.make_async_remote_copy(
            src_ref=own.at[pl.ds(lo, size)], dst_ref=land_r.at[pl.ds(lo, size)],
            send_sem=send_l.at[c], recv_sem=recv_r.at[c],
            device_id=(leaf - 1, samp), device_id_type=MESH,
        )

    @pl.when(leaf < n_leaf - 1)
    def _():
        to_right(0, half, half).start()

    @pl.when(leaf > 0)
    def _():
        to_left(0, 0, half).start()

    def send_pair(j, carry):
        @pl.when(leaf < n_leaf - 1)
        def _():
            to_right(j + 1, half - 1 - j).start()

        @pl.when(leaf > 0)
        def _():
            to_left(j + 1, half + j).start()

        return carry

    lax.fori_loop(0, steps, send_pair, 0)

    for r in range(rank * rank // 128):
        for src, dst in ((inner_ref, inner_v), (upper_ref, upper_v)):
            count = src.shape[0]
            tile = src[:, 128 * r:128 * r + 128].astype(F32)
            dst[pl.ds(2 * r, count, stride=rank), :] = tile
            dst[pl.ds(2 * r + 1, count, stride=rank), :] = pltpu.roll(tile, 64, 1)

    eye = (
        lax.broadcasted_iota(jnp.int32, (rank, rank), 0)
        == lax.broadcasted_iota(jnp.int32, (rank, rank), 1)
    ).astype(F32)
    rows = None
    starts = []
    offset = 0
    for h in range(heights):
        starts.append(offset)
        offset += n_leaf >> h
    for h in reversed(range(heights)):
        node = starts[h] + lax.shift_right_logical(leaf, h)
        mat = upper_v[pl.ds(pl.multiple_of(node * rank, rank), rank), :][:, :rank].astype(BF16)
        rows = eye if rows is None else jnp.concatenate([eye, rows], axis=0)
        rows = chain_step(rows, mat)
    rows_high, rows_low = split(rows)
    ascend[...] = jnp.concatenate([rows_high, rows_high, rows_low], axis=1)
    paths[nodes] = eye

    def children(q):
        mats = inner_v[pl.ds(pl.multiple_of(q * 2 * rank, 2 * rank), 2 * rank), :]
        return chain_step(paths[leaf_count + q], mats[:, :rank].astype(BF16))

    def inner_pair(i, carry):
        q = leaf_count - 2 - i
        both = children(q)
        paths[2 * q] = both[:, :rank]
        paths[2 * q + 1] = pltpu.roll(both, 64, 1)[:, :rank]
        return carry

    lax.fori_loop(0, pairs - 1, inner_pair, 0)

    def leaf_pair(q, carry):
        high, low = split(children(q))
        leaf_path[q] = jnp.concatenate([high, high, low], axis=1)
        return carry

    lax.fori_loop(0, pairs, leaf_pair, 0, unroll=4)

    load_samples.wait()

    def pack_samples(u, carry):
        packed[u] = pair_tile(samples_v, u)
        return carry

    lax.fori_loop(0, pairs, pack_samples, 0, unroll=4)
    up_acc[...] = jnp.zeros_like(up_acc)
    load_basis.wait()
    load_near.wait()

    lane_half = lax.broadcasted_iota(jnp.int32, (1, 128), 1) // 64
    lower = lax.broadcasted_iota(jnp.int32, (leaf_size, 128), 1) < 64
    base = leaf * leaf_count - leaf_count

    def near_product(p):
        tiles = []
        for k in range(slots):
            at = jnp.clip(index_ref[k, p] - base, 0, 3 * leaf_count - 1)
            want = jnp.where(k < count_ref[p], at & 1, 2)
            mask = (lane_half == want).astype(F32).astype(BF16)
            tiles.append(held[lax.shift_right_logical(at, 1)] * mask)
        left = jnp.concatenate([near_v[p, k] for k in range(slots)], axis=1)
        total = dot(left, jnp.concatenate(tiles, axis=0))
        return total + pltpu.roll(total, 64, 1)

    def process(u, w):
        near = jnp.where(lower, near_product(2 * u), near_product(2 * u + 1))
        far = (packed[u].astype(F32) - near).astype(BF16)
        basis = basis_v[pl.ds(2 * u, 2)].reshape(2 * rank, leaf_size)
        both = dot(basis, far)
        top, bottom = both[:rank], both[rank:]
        coeff_v[2 * u] = top[:, :width]
        coeff_v[2 * u + 1] = pltpu.roll(bottom, 64, 1)[:, :width]
        low_lane = lower[:rank]
        top = jnp.where(low_lane, top, 0.0)
        bottom = jnp.where(low_lane, 0.0, bottom)
        top_high, top_low = split(top)
        bottom_high, bottom_low = split(bottom)
        block_high = jnp.concatenate([top_high, bottom_high], axis=0)
        block_low = jnp.concatenate([top_low, bottom_low], axis=0)
        row_high = top_high + bottom_high
        row_low = top_low + bottom_low
        gram = dot_nt(
            jnp.concatenate([row_high, row_high, row_low], axis=1),
            jnp.concatenate([block_high, block_low, block_high], axis=1),
        ) * (1.0 / total_columns)
        for t in range(n_samp):
            gram_send[t, pl.ds(pl.multiple_of(w * part, part), part), :] = (
                gram[t * part:(t + 1) * part].astype(gram_send.dtype)
            )
        return dot(leaf_path[u], jnp.concatenate([block_high, block_low, block_high], axis=0))

    def accept(land, at_held, lo, size):
        def body(i, carry):
            held[at_held + lo + i] = land[lo + i]
            return carry

        lax.fori_loop(0, size, body, 0)

    @pl.when(leaf > 0)
    def _():
        to_right(0, half, half).wait_recv()
        accept(land_l, 0, half, half)

    @pl.when(leaf < n_leaf - 1)
    def _():
        to_left(0, 0, half).wait_recv()
        accept(land_r, 2 * pairs, 0, half)

    span = 2 * part

    def gram_copy(d, j):
        at = pl.ds(pl.multiple_of(j * span, span), span)
        return pltpu.make_async_remote_copy(
            src_ref=gram_send.at[samp ^ d, at], dst_ref=gram_recv.at[d - 1, at],
            send_sem=gram_ssem.at[d - 1, j], recv_sem=gram_rsem.at[d - 1, j],
            device_id=(leaf, samp ^ d), device_id_type=MESH,
        )

    def out_copy(j, side):
        at = pl.ds(2 * (half - 1 - j) if side == 0 else 2 * (half + j), 2)
        return pltpu.make_async_copy(coeff_v.at[at], coeff_hbm.at[at], out_sem.at[side, j])

    def step(j, carry):
        lo_l = half - 1 - j
        lo_r = half + j

        @pl.when(leaf > 0)
        def _():
            to_right(j + 1, lo_l).wait_recv()
            held[lo_l] = land_l[lo_l]

        @pl.when(leaf < n_leaf - 1)
        def _():
            to_left(j + 1, lo_r).wait_recv()
            held[2 * pairs + lo_r] = land_r[lo_r]

        up_acc[...] += process(lo_l, 2 * j) + process(lo_r, 2 * j + 1)
        for d in range(1, n_samp):
            gram_copy(d, j).start()
        out_copy(j, 0).start()
        out_copy(j, 1).start()
        return carry

    lax.fori_loop(0, steps, step, 0)

    total = up_acc[...]
    total_high, total_low = split(total + pltpu.roll(total, 64, 1))
    total = dot(ascend[...], jnp.concatenate([total_high, total_low, total_high], axis=0))
    side = rank // 2
    for h in range(heights):
        up_send[h * side:(h + 1) * side] = jnp.where(
            lower[:side], total[h * rank:h * rank + side], total[h * rank + side:(h + 1) * rank]
        )

    def up_copy(d):
        first = (d.bit_length() - 1) * side
        at = pl.ds(first, heights * side - first)
        return pltpu.make_async_remote_copy(
            src_ref=up_send.at[at], dst_ref=up_recv.at[d - 1, at],
            send_sem=up_ssem.at[d - 1], recv_sem=up_rsem.at[d - 1],
            device_id=(leaf ^ d, samp), device_id_type=MESH,
        )

    for d in range(1, n_leaf):
        up_copy(d).start()

    def gram_wait(j, carry):
        for d in range(1, n_samp):
            gram_copy(d, j).wait_recv()
        return carry

    lax.fori_loop(0, steps, gram_wait, 0)
    for w in range(pairs):
        u = half - 1 - w // 2 if w % 2 == 0 else half + w // 2
        at = slice(w * part, (w + 1) * part)
        value = gram_send[samp, at, :].astype(F32)
        for d in range(1, n_samp):
            value = value + gram_recv[d - 1, at, :].astype(F32)
        gram_sum[u * part:(u + 1) * part, :] = value
    low16 = lower[:pairs]
    for m in range(part // 2):
        first = gram_sum[pl.ds(2 * m, pairs, stride=part), :]
        second = gram_sum[pl.ds(2 * m + 1, pairs, stride=part), :]
        even = jnp.where(low16, first, pltpu.roll(second, 64, 1))
        odd = jnp.where(low16, pltpu.roll(first, 64, 1), second)
        lo = m * leaf_count
        gram_mix[pl.ds(lo, pairs, stride=2), :] = even
        gram_mix[pl.ds(lo + 1, pairs, stride=2), :] = odd
        gram_ref[:, 128 * m:128 * m + 128] = gram_mix[lo:lo + leaf_count, :]

    for d in range(1, n_leaf):
        up_copy(d).wait_recv()
    for h in range(heights):
        at = slice(h * side, (h + 1) * side)
        value = up_send[at, :]
        for d in range(1, n_leaf):
            if d.bit_length() <= h + 1:
                value = value + up_recv[d - 1, at, :]
        ancestor_ref[h, 0:side, :] = value[:, :width]
        ancestor_ref[h, side:rank, :] = pltpu.roll(value, 64, 1)[:, :width]

    @pl.when(leaf < n_leaf - 1)
    def _():
        to_right(0, half, half).wait_send()

    @pl.when(leaf > 0)
    def _():
        to_left(0, 0, half).wait_send()

    def finish(j, carry):
        @pl.when(leaf < n_leaf - 1)
        def _():
            to_right(j + 1, half - 1 - j).wait_send()

        @pl.when(leaf > 0)
        def _():
            to_left(j + 1, half + j).wait_send()

        for d in range(1, n_samp):
            gram_copy(d, j).wait_send()
        out_copy(j, 0).wait()
        out_copy(j, 1).wait()
        return carry

    lax.fori_loop(0, steps, finish, 0)
    for d in range(1, n_leaf):
        up_copy(d).wait_send()


def deliver(count, *refs):
    sources, targets, sems = refs[:count], refs[count:-1], refs[-1]
    copies = [
        pltpu.make_async_copy(source, target, sems.at[i])
        for i, (source, target) in enumerate(zip(sources, targets))
    ]
    for copy in copies:
        copy.start()
    for copy in copies:
        copy.wait()


def shards(
    n_leaf, n_samp,
    samples, omega, leaf_basis, near_blocks, near_index, near_count, inner_transfer, upper_transfer
):
    leaf_count, rank, leaf_size = leaf_basis.shape
    width = samples.shape[1]
    pairs = leaf_count // 2
    steps = pairs // 2
    heights = n_leaf.bit_length() - 1
    part = rank // n_samp
    nodes = inner_transfer.shape[0]
    upper_nodes = upper_transfer.shape[0]
    wire = BF16 if part % 16 == 0 else F32
    omega, samples, near_index = omega.T, samples.T, near_index.T
    vmem = pl.BlockSpec(memory_space=pltpu.VMEM)
    smem = pl.BlockSpec(memory_space=pltpu.SMEM)
    hbm = pl.BlockSpec(memory_space=pl.ANY)
    dma = pltpu.SemaphoreType.DMA
    coeffs, gram, ancestors = pl.pallas_call(
        functools.partial(kernel, n_leaf, n_samp, width * n_samp),
        out_shape=(
            jax.ShapeDtypeStruct((leaf_count, rank, width), F32),
            jax.ShapeDtypeStruct((leaf_count, part * rank), F32),
            jax.ShapeDtypeStruct((heights, rank, width), F32),
        ),
        in_specs=[smem, smem, vmem, vmem, hbm, hbm, hbm, hbm],
        out_specs=(hbm, vmem, vmem),
        scratch_shapes=[
            pltpu.VMEM(omega.shape, BF16),
            pltpu.VMEM(samples.shape, BF16),
            pltpu.VMEM(leaf_basis.shape, BF16),
            pltpu.VMEM(near_blocks.shape, BF16),
            pltpu.VMEM((pairs, leaf_size, 128), BF16),
            pltpu.VMEM((pairs, leaf_size, 128), BF16),
            pltpu.VMEM((pairs, leaf_size, 128), BF16),
            pltpu.VMEM((3 * pairs, leaf_size, 128), BF16),
            pltpu.VMEM((pairs, leaf_size, 128), BF16),
            pltpu.VMEM((nodes * rank, 128), F32),
            pltpu.VMEM((upper_nodes * rank, 128), F32),
            pltpu.VMEM((nodes + 1, rank, rank), F32),
            pltpu.VMEM((heights * rank, 3 * rank), BF16),
            pltpu.VMEM((pairs, rank, 384), BF16),
            pltpu.VMEM((rank, 128), F32),
            pltpu.VMEM((heights * rank // 2, 128), F32),
            pltpu.VMEM((n_leaf - 1, heights * rank // 2, 128), F32),
            pltpu.VMEM((n_samp, pairs * part, 128), wire),
            pltpu.VMEM((n_samp - 1, pairs * part, 128), wire),
            pltpu.VMEM((pairs * part, 128), F32),
            pltpu.VMEM((part // 2 * leaf_count, 128), F32),
            pltpu.VMEM((leaf_count, rank, width), F32),
            dma((3,)), dma,
            dma((steps + 1,)), dma((steps + 1,)), dma((steps + 1,)), dma((steps + 1,)),
            dma((n_samp - 1, steps)), dma((n_samp - 1, steps)),
            dma((n_leaf - 1,)), dma((n_leaf - 1,)),
            dma((2, steps)),
        ],
        compiler_params=pltpu.CompilerParams(
            collective_id=0, has_side_effects=True, vmem_limit_bytes=56 * 1024 * 1024
        ),
    )(near_index, near_count, inner_transfer, upper_transfer, omega, samples, leaf_basis, near_blocks)
    results = (coeffs, gram, ancestors[None])
    return pl.pallas_call(
        functools.partial(deliver, len(results)),
        out_shape=tuple(jax.ShapeDtypeStruct(x.shape, x.dtype) for x in results),
        in_specs=[hbm] * len(results),
        out_specs=(hbm,) * len(results),
        scratch_shapes=[dma((len(results),))],
        compiler_params=pltpu.CompilerParams(vmem_limit_bytes=62 * 1024 * 1024),
    )(*results)


def solution(mesh):
    return jax.shard_map(
        functools.partial(shards, mesh.shape["leaf"], mesh.shape["samp"]),
        mesh=mesh,
        in_specs=(
            P("leaf", "samp"),
            P("leaf", "samp"),
            P("leaf", None, None),
            P("leaf", None, None, None),
            P("leaf", None),
            P("leaf"),
            P("leaf", None),
            P(),
        ),
        out_specs=(P("leaf", None, "samp"), P("leaf", "samp"), P("leaf", None, None, "samp")),
        check_vma=False,
    )
```

```python
import functools

import jax
import jax.numpy as jnp
from jax import lax
from jax.experimental import pallas as pl
from jax.experimental.pallas import tpu as pltpu
from jax.sharding import PartitionSpec as P

MESH = pl.DeviceIdType.MESH
F32 = jnp.float32
BF16 = jnp.bfloat16


def split(x):
    high = x.astype(BF16)
    return high, (x - high.astype(F32)).astype(BF16)


def dot_nt(a, b):
    return lax.dot_general(a, b, (((1,), (1,)), ((), ())), preferred_element_type=F32)


def dot(a, b):
    return jnp.dot(a, b, preferred_element_type=F32)


def chain_step(rows, mats):
    high, low = split(rows)
    n = rows.shape[0]
    both = dot_nt(jnp.concatenate([high, low], axis=0), mats)
    return both[:n] + both[n:]


def kernel(
    n_leaf, n_samp, total_columns,
    index_ref, count_ref, inner_ref, upper_ref, omega_hbm, samples_hbm, basis_hbm, near_hbm,
    coeff_hbm, gram_ref, ancestor_ref,
    omega_v, samples_v, basis_v, near_v, land_l, land_r, held,
    inner_v, upper_v, paths, ascend, leaf_path, up_acc, up_send, up_recv,
    gram_send, gram_recv, gram_sum, gram_mix, coeff_v,
    load_sem, near_sem, send_l, send_r, recv_l, recv_r,
    gram_ssem, gram_rsem, up_ssem, up_rsem, out_sem,
):
    leaf = lax.axis_index("leaf")
    samp = lax.axis_index("samp")
    leaf_count, rank, leaf_size = basis_v.shape
    slots = near_v.shape[1]
    width = omega_v.shape[0]
    pairs = leaf_count // 2
    half = pairs // 2
    heights = ancestor_ref.shape[0]
    steps = half
    part = rank // n_samp
    nodes = inner_ref.shape[0]

    load_omega = pltpu.make_async_copy(omega_hbm, omega_v, load_sem.at[0])
    load_samples = pltpu.make_async_copy(samples_hbm, samples_v, load_sem.at[1])
    load_basis = pltpu.make_async_copy(basis_hbm, basis_v, load_sem.at[2])
    load_near = pltpu.make_async_copy(near_hbm, near_v, near_sem)
    load_omega.start()
    load_samples.start()
    load_basis.start()
    load_near.start()

    barrier = pltpu.get_barrier_semaphore()
    for d in range(1, n_leaf):
        pl.semaphore_signal(barrier, inc=1, device_id=(leaf ^ d, samp), device_id_type=MESH)
    for d in range(1, n_samp):
        pl.semaphore_signal(barrier, inc=1, device_id=(leaf, samp ^ d), device_id_type=MESH)

    pl.semaphore_wait(barrier, n_leaf + n_samp - 2)

    def lanes(lo, size=1):
        unit = 2 * leaf_size
        return pl.ds(pl.multiple_of(lo * unit, unit), size * unit)

    def to_right(c, lo, size=1):
        return pltpu.make_async_remote_copy(
            src_ref=omega_hbm.at[:, lanes(lo, size)], dst_ref=land_l.at[:, lanes(lo, size)],
            send_sem=send_r.at[c], recv_sem=recv_l.at[c],
            device_id=(leaf + 1, samp), device_id_type=MESH,
        )

    def to_left(c, lo, size=1):
        return pltpu.make_async_remote_copy(
            src_ref=omega_hbm.at[:, lanes(lo, size)], dst_ref=land_r.at[:, lanes(lo, size)],
            send_sem=send_l.at[c], recv_sem=recv_r.at[c],
            device_id=(leaf - 1, samp), device_id_type=MESH,
        )

    @pl.when(leaf < n_leaf - 1)
    def _():
        to_right(0, half, half).start()

    @pl.when(leaf > 0)
    def _():
        to_left(0, 0, half).start()

    def send_pair(j, carry):
        @pl.when(leaf < n_leaf - 1)
        def _():
            to_right(j + 1, half - 1 - j).start()

        @pl.when(leaf > 0)
        def _():
            to_left(j + 1, half + j).start()

        return carry

    lax.fori_loop(0, steps, send_pair, 0)

    for r in range(rank * rank // 128):
        for src, dst in ((inner_ref, inner_v), (upper_ref, upper_v)):
            count = src.shape[0]
            tile = src[:, 128 * r:128 * r + 128].astype(F32)
            dst[pl.ds(2 * r, count, stride=rank), :] = tile
            dst[pl.ds(2 * r + 1, count, stride=rank), :] = pltpu.roll(tile, 64, 1)

    eye = (
        lax.broadcasted_iota(jnp.int32, (rank, rank), 0)
        == lax.broadcasted_iota(jnp.int32, (rank, rank), 1)
    ).astype(F32)
    rows = None
    starts = []
    offset = 0
    for h in range(heights):
        starts.append(offset)
        offset += n_leaf >> h
    for h in reversed(range(heights)):
        node = starts[h] + lax.shift_right_logical(leaf, h)
        mat = upper_v[pl.ds(pl.multiple_of(node * rank, rank), rank), :][:, :rank].astype(BF16)
        rows = eye if rows is None else jnp.concatenate([eye, rows], axis=0)
        rows = chain_step(rows, mat)
    rows_high, rows_low = split(rows)
    ascend[...] = jnp.concatenate([rows_high, rows_high, rows_low], axis=1)
    paths[nodes] = eye

    def children(q):
        mats = inner_v[pl.ds(pl.multiple_of(q * 2 * rank, 2 * rank), 2 * rank), :]
        return chain_step(paths[leaf_count + q], mats[:, :rank].astype(BF16))

    def inner_pair(i, carry):
        q = leaf_count - 2 - i
        both = children(q)
        paths[2 * q] = both[:, :rank]
        paths[2 * q + 1] = pltpu.roll(both, 64, 1)[:, :rank]
        return carry

    lax.fori_loop(0, pairs - 1, inner_pair, 0)

    def leaf_pair(q, carry):
        high, low = split(children(q))
        leaf_path[q] = jnp.concatenate([high, high, low], axis=1)
        return carry

    lax.fori_loop(0, pairs, leaf_pair, 0, unroll=4)

    def accept(src, at_held, lo):
        both = src[:, lanes(lo)]
        held[at_held + 2 * lo] = both[:, :leaf_size]
        held[at_held + 2 * lo + 1] = both[:, leaf_size:]

    def accept_many(src, at_held, lo, size):
        def body(i, carry):
            accept(src, at_held, lo + i)
            return carry

        lax.fori_loop(0, size, body, 0, unroll=4)

    load_omega.wait()
    accept_many(omega_v, leaf_count, 0, pairs)
    up_acc[...] = jnp.zeros_like(up_acc)
    load_samples.wait()
    load_basis.wait()
    load_near.wait()

    lower = lax.broadcasted_iota(jnp.int32, (leaf_size, 128), 1) < 64
    base = leaf * leaf_count - leaf_count

    def near_product(p):
        tiles = []
        for k in range(slots):
            at = jnp.clip(index_ref[k, p] - base, 0, 3 * leaf_count - 1)
            live = jnp.where(k < count_ref[p], 1.0, 0.0)
            tiles.append(held[at] * jnp.full((1, leaf_size), live, F32).astype(BF16))
        blocks = jnp.concatenate([near_v[p, k] for k in range(slots)], axis=1)
        return dot_nt(jnp.concatenate(tiles, axis=1), blocks)

    def process(u, w):
        near = jnp.concatenate([near_product(2 * u), near_product(2 * u + 1)], axis=0)
        mine = samples_v[:, lanes(u)]
        mine = jnp.concatenate([mine[:, :leaf_size], mine[:, leaf_size:]], axis=0)
        far = (mine.astype(F32) - near).astype(BF16)
        basis = basis_v[pl.ds(2 * u, 2)].reshape(2 * rank, leaf_size)
        both = dot_nt(basis, far)
        top, bottom = both[:rank], both[rank:]
        coeff_v[2 * u] = top[:, :width]
        coeff_v[2 * u + 1] = pltpu.roll(bottom, 64, 1)[:, :width]
        low_lane = lower[:rank]
        top = jnp.where(low_lane, top, 0.0)
        bottom = jnp.where(low_lane, 0.0, bottom)
        top_high, top_low = split(top)
        bottom_high, bottom_low = split(bottom)
        block_high = jnp.concatenate([top_high, bottom_high], axis=0)
        block_low = jnp.concatenate([top_low, bottom_low], axis=0)
        row_high = top_high + bottom_high
        row_low = top_low + bottom_low
        gram = dot_nt(
            jnp.concatenate([row_high, row_high, row_low], axis=1),
            jnp.concatenate([block_high, block_low, block_high], axis=1),
        ) * (1.0 / total_columns)
        for t in range(n_samp):
            gram_send[t, pl.ds(pl.multiple_of(w * part, part), part), :] = (
                gram[t * part:(t + 1) * part].astype(gram_send.dtype)
            )
        return dot(leaf_path[u], jnp.concatenate([block_high, block_low, block_high], axis=0))

    @pl.when(leaf > 0)
    def _():
        to_right(0, half, half).wait_recv()
        accept_many(land_l, 0, half, half)

    @pl.when(leaf < n_leaf - 1)
    def _():
        to_left(0, 0, half).wait_recv()
        accept_many(land_r, 2 * leaf_count, 0, half)

    span = 2 * part

    def gram_copy(d, j):
        at = pl.ds(pl.multiple_of(j * span, span), span)
        return pltpu.make_async_remote_copy(
            src_ref=gram_send.at[samp ^ d, at], dst_ref=gram_recv.at[d - 1, at],
            send_sem=gram_ssem.at[d - 1, j], recv_sem=gram_rsem.at[d - 1, j],
            device_id=(leaf, samp ^ d), device_id_type=MESH,
        )

    def out_copy(j, side):
        at = pl.ds(2 * (half - 1 - j) if side == 0 else 2 * (half + j), 2)
        return pltpu.make_async_copy(coeff_v.at[at], coeff_hbm.at[at], out_sem.at[side, j])

    def step(j, carry):
        lo_l = half - 1 - j
        lo_r = half + j

        @pl.when(leaf > 0)
        def _():
            to_right(j + 1, lo_l).wait_recv()
            accept(land_l, 0, lo_l)

        @pl.when(leaf < n_leaf - 1)
        def _():
            to_left(j + 1, lo_r).wait_recv()
            accept(land_r, 2 * leaf_count, lo_r)

        up_acc[...] += process(lo_l, 2 * j) + process(lo_r, 2 * j + 1)
        for d in range(1, n_samp):
            gram_copy(d, j).start()
        out_copy(j, 0).start()
        out_copy(j, 1).start()
        return carry

    lax.fori_loop(0, steps, step, 0)

    total = up_acc[...]
    total_high, total_low = split(total + pltpu.roll(total, 64, 1))
    total = dot(ascend[...], jnp.concatenate([total_high, total_low, total_high], axis=0))
    side = rank // 2
    for h in range(heights):
        up_send[h * side:(h + 1) * side] = jnp.where(
            lower[:side], total[h * rank:h * rank + side], total[h * rank + side:(h + 1) * rank]
        )

    def up_copy(d):
        first = (d.bit_length() - 1) * side
        at = pl.ds(first, heights * side - first)
        return pltpu.make_async_remote_copy(
            src_ref=up_send.at[at], dst_ref=up_recv.at[d - 1, at],
            send_sem=up_ssem.at[d - 1], recv_sem=up_rsem.at[d - 1],
            device_id=(leaf ^ d, samp), device_id_type=MESH,
        )

    for d in range(1, n_leaf):
        up_copy(d).start()

    def gram_wait(j, carry):
        for d in range(1, n_samp):
            gram_copy(d, j).wait_recv()
        return carry

    lax.fori_loop(0, steps, gram_wait, 0)
    for w in range(pairs):
        u = half - 1 - w // 2 if w % 2 == 0 else half + w // 2
        at = slice(w * part, (w + 1) * part)
        value = gram_send[samp, at, :].astype(F32)
        for d in range(1, n_samp):
            value = value + gram_recv[d - 1, at, :].astype(F32)
        gram_sum[u * part:(u + 1) * part, :] = value
    low16 = lower[:pairs]
    for m in range(part // 2):
        first = gram_sum[pl.ds(2 * m, pairs, stride=part), :]
        second = gram_sum[pl.ds(2 * m + 1, pairs, stride=part), :]
        even = jnp.where(low16, first, pltpu.roll(second, 64, 1))
        odd = jnp.where(low16, pltpu.roll(first, 64, 1), second)
        lo = m * leaf_count
        gram_mix[pl.ds(lo, pairs, stride=2), :] = even
        gram_mix[pl.ds(lo + 1, pairs, stride=2), :] = odd
        gram_ref[:, 128 * m:128 * m + 128] = gram_mix[lo:lo + leaf_count, :]

    for d in range(1, n_leaf):
        up_copy(d).wait_recv()
    for h in range(heights):
        at = slice(h * side, (h + 1) * side)
        value = up_send[at, :]
        for d in range(1, n_leaf):
            if d.bit_length() <= h + 1:
                value = value + up_recv[d - 1, at, :]
        ancestor_ref[h, 0:side, :] = value[:, :width]
        ancestor_ref[h, side:rank, :] = pltpu.roll(value, 64, 1)[:, :width]

    @pl.when(leaf < n_leaf - 1)
    def _():
        to_right(0, half, half).wait_send()

    @pl.when(leaf > 0)
    def _():
        to_left(0, 0, half).wait_send()

    def finish(j, carry):
        @pl.when(leaf < n_leaf - 1)
        def _():
            to_right(j + 1, half - 1 - j).wait_send()

        @pl.when(leaf > 0)
        def _():
            to_left(j + 1, half + j).wait_send()

        for d in range(1, n_samp):
            gram_copy(d, j).wait_send()
        out_copy(j, 0).wait()
        out_copy(j, 1).wait()
        return carry

    lax.fori_loop(0, steps, finish, 0)
    for d in range(1, n_leaf):
        up_copy(d).wait_send()


def deliver(count, *refs):
    sources, targets, rooms = refs[:count], refs[count:2 * count], refs[2 * count:3 * count]
    sems = refs[-1]
    reads = [pltpu.make_async_copy(sources[i], rooms[i], sems.at[0, i]) for i in range(count)]
    writes = [pltpu.make_async_copy(rooms[i], targets[i], sems.at[1, i]) for i in range(count)]
    for read in reads:
        read.start()
    for read, write in zip(reads, writes):
        read.wait()
        write.start()
    for write in writes:
        write.wait()


def shards(
    n_leaf, n_samp,
    samples, omega, leaf_basis, near_blocks, near_index, near_count, inner_transfer, upper_transfer
):
    leaf_count, rank, leaf_size = leaf_basis.shape
    width = samples.shape[1]
    pairs = leaf_count // 2
    steps = pairs // 2
    heights = n_leaf.bit_length() - 1
    part = rank // n_samp
    nodes = inner_transfer.shape[0]
    upper_nodes = upper_transfer.shape[0]
    wire = BF16 if part % 16 == 0 else F32
    omega, samples, near_index = omega.T, samples.T, near_index.T
    vmem = pl.BlockSpec(memory_space=pltpu.VMEM)
    smem = pl.BlockSpec(memory_space=pltpu.SMEM)
    hbm = pl.BlockSpec(memory_space=pl.ANY)
    dma = pltpu.SemaphoreType.DMA
    coeffs, gram, ancestors = pl.pallas_call(
        functools.partial(kernel, n_leaf, n_samp, width * n_samp),
        out_shape=(
            jax.ShapeDtypeStruct((leaf_count, rank, width), F32),
            jax.ShapeDtypeStruct((leaf_count, part * rank), F32),
            jax.ShapeDtypeStruct((heights, rank, width), F32),
        ),
        in_specs=[smem, smem, vmem, vmem, hbm, hbm, hbm, hbm],
        out_specs=(hbm, vmem, vmem),
        scratch_shapes=[
            pltpu.VMEM(omega.shape, BF16),
            pltpu.VMEM(samples.shape, BF16),
            pltpu.VMEM(leaf_basis.shape, BF16),
            pltpu.VMEM(near_blocks.shape, BF16),
            pltpu.VMEM(omega.shape, BF16),
            pltpu.VMEM(omega.shape, BF16),
            pltpu.VMEM((3 * leaf_count, width, leaf_size), BF16),
            pltpu.VMEM((nodes * rank, 128), F32),
            pltpu.VMEM((upper_nodes * rank, 128), F32),
            pltpu.VMEM((nodes + 1, rank, rank), F32),
            pltpu.VMEM((heights * rank, 3 * rank), BF16),
            pltpu.VMEM((pairs, rank, 384), BF16),
            pltpu.VMEM((rank, 128), F32),
            pltpu.VMEM((heights * rank // 2, 128), F32),
            pltpu.VMEM((n_leaf - 1, heights * rank // 2, 128), F32),
            pltpu.VMEM((n_samp, pairs * part, 128), wire),
            pltpu.VMEM((n_samp - 1, pairs * part, 128), wire),
            pltpu.VMEM((pairs * part, 128), F32),
            pltpu.VMEM((part // 2 * leaf_count, 128), F32),
            pltpu.VMEM((leaf_count, rank, width), F32),
            dma((3,)), dma,
            dma((steps + 1,)), dma((steps + 1,)), dma((steps + 1,)), dma((steps + 1,)),
            dma((n_samp - 1, steps)), dma((n_samp - 1, steps)),
            dma((n_leaf - 1,)), dma((n_leaf - 1,)),
            dma((2, steps)),
        ],
        compiler_params=pltpu.CompilerParams(
            collective_id=0, has_side_effects=True, vmem_limit_bytes=56 * 1024 * 1024
        ),
    )(near_index, near_count, inner_transfer, upper_transfer, omega, samples, leaf_basis, near_blocks)
    results = (coeffs, gram, ancestors[None])
    return pl.pallas_call(
        functools.partial(deliver, len(results)),
        out_shape=tuple(jax.ShapeDtypeStruct(x.shape, x.dtype) for x in results),
        in_specs=[hbm] * len(results),
        out_specs=(hbm,) * len(results),
        scratch_shapes=[pltpu.VMEM(x.shape, x.dtype) for x in results] + [dma((2, len(results)))],
        compiler_params=pltpu.CompilerParams(vmem_limit_bytes=62 * 1024 * 1024),
    )(*results)


def solution(mesh):
    return jax.shard_map(
        functools.partial(shards, mesh.shape["leaf"], mesh.shape["samp"]),
        mesh=mesh,
        in_specs=(
            P("leaf", "samp"),
            P("leaf", "samp"),
            P("leaf", None, None),
            P("leaf", None, None, None),
            P("leaf", None),
            P("leaf"),
            P("leaf", None),
            P(),
        ),
        out_specs=(P("leaf", None, "samp"), P("leaf", "samp"), P("leaf", None, None, "samp")),
        check_vma=False,
    )
```

```python
import functools

import jax
import jax.numpy as jnp
from jax import lax
from jax.experimental import pallas as pl
from jax.experimental.pallas import tpu as pltpu
from jax.sharding import PartitionSpec as P

MESH = pl.DeviceIdType.MESH
F32 = jnp.float32
BF16 = jnp.bfloat16


def split(x):
    high = x.astype(BF16)
    return high, (x - high.astype(F32)).astype(BF16)


def dot_nt(a, b):
    return lax.dot_general(a, b, (((1,), (1,)), ((), ())), preferred_element_type=F32)


def dot(a, b):
    return jnp.dot(a, b, preferred_element_type=F32)


def chain_step(rows, mats):
    high, low = split(rows)
    n = rows.shape[0]
    both = dot_nt(jnp.concatenate([high, low], axis=0), mats)
    return both[:n] + both[n:]


def kernel(
    n_leaf, n_samp, total_columns,
    index_ref, count_ref, inner_ref, upper_ref, omega_hbm, samples_hbm, basis_hbm, near_hbm,
    coeff_hbm, gram_ref, ancestor_ref,
    omega_v, samples_v, basis_v, near_v, land_l, land_r, held,
    inner_v, upper_v, paths, ascend, leaf_path, up_acc, up_send, up_recv,
    gram_send, gram_recv, gram_sum, gram_mix, coeff_v,
    load_sem, near_sem, send_l, send_r, recv_l, recv_r,
    gram_ssem, gram_rsem, up_ssem, up_rsem, out_sem,
):
    leaf = lax.axis_index("leaf")
    samp = lax.axis_index("samp")
    leaf_count, rank, leaf_size = basis_v.shape
    slots = near_v.shape[1]
    width = omega_v.shape[0]
    pairs = leaf_count // 2
    half = pairs // 2
    heights = ancestor_ref.shape[0]
    steps = half
    part = rank // n_samp
    nodes = inner_ref.shape[0]

    load_omega = pltpu.make_async_copy(omega_hbm, omega_v, load_sem.at[0])
    load_samples = pltpu.make_async_copy(samples_hbm, samples_v, load_sem.at[1])
    load_basis = pltpu.make_async_copy(basis_hbm, basis_v, load_sem.at[2])
    load_near = pltpu.make_async_copy(near_hbm, near_v, near_sem)
    load_omega.start()
    load_samples.start()
    load_basis.start()
    load_near.start()

    barrier = pltpu.get_barrier_semaphore()
    for d in range(1, n_leaf):
        pl.semaphore_signal(barrier, inc=1, device_id=(leaf ^ d, samp), device_id_type=MESH)
    for d in range(1, n_samp):
        pl.semaphore_signal(barrier, inc=1, device_id=(leaf, samp ^ d), device_id_type=MESH)

    pl.semaphore_wait(barrier, n_leaf + n_samp - 2)

    def lanes(pair):
        unit = 2 * leaf_size
        return pl.ds(pl.multiple_of(pair * unit, unit), unit)

    def to_right(c):
        at = lanes(pairs - 1 - c)
        return pltpu.make_async_remote_copy(
            src_ref=omega_hbm.at[:, at], dst_ref=land_l.at[:, at],
            send_sem=send_r.at[c], recv_sem=recv_l.at[c],
            device_id=(leaf + 1, samp), device_id_type=MESH,
        )

    def to_left(c):
        at = lanes(c)
        return pltpu.make_async_remote_copy(
            src_ref=omega_hbm.at[:, at], dst_ref=land_r.at[:, at],
            send_sem=send_l.at[c], recv_sem=recv_r.at[c],
            device_id=(leaf - 1, samp), device_id_type=MESH,
        )

    def send(c):
        @pl.when(leaf < n_leaf - 1)
        def _():
            to_right(c).start()

        @pl.when(leaf > 0)
        def _():
            to_left(c).start()

    window = 4

    def pump(c):
        @pl.when(leaf < n_leaf - 1)
        def _():
            to_right(c).wait_send()

        @pl.when(leaf > 0)
        def _():
            to_left(c).wait_send()

        @pl.when(c + window < pairs)
        def _():
            send(c + window)

    for c in range(window):
        send(c)

    lines = rank * rank // 128
    for r in range(lines):
        if r % (lines // 2) == 0 and r > 0:
            pump(r // (lines // 2) - 1)
        for src, dst in ((inner_ref, inner_v), (upper_ref, upper_v)):
            count = src.shape[0]
            tile = src[:, 128 * r:128 * r + 128].astype(F32)
            dst[pl.ds(2 * r, count, stride=rank), :] = tile
            dst[pl.ds(2 * r + 1, count, stride=rank), :] = pltpu.roll(tile, 64, 1)

    pump(1)

    eye = (
        lax.broadcasted_iota(jnp.int32, (rank, rank), 0)
        == lax.broadcasted_iota(jnp.int32, (rank, rank), 1)
    ).astype(F32)
    rows = None
    starts = []
    offset = 0
    for h in range(heights):
        starts.append(offset)
        offset += n_leaf >> h
    for h in reversed(range(heights)):
        node = starts[h] + lax.shift_right_logical(leaf, h)
        mat = upper_v[pl.ds(pl.multiple_of(node * rank, rank), rank), :][:, :rank].astype(BF16)
        rows = eye if rows is None else jnp.concatenate([eye, rows], axis=0)
        rows = chain_step(rows, mat)
    rows_high, rows_low = split(rows)
    ascend[...] = jnp.concatenate([rows_high, rows_high, rows_low], axis=1)
    paths[nodes] = eye

    def children(q):
        mats = inner_v[pl.ds(pl.multiple_of(q * 2 * rank, 2 * rank), 2 * rank), :]
        return chain_step(paths[leaf_count + q], mats[:, :rank].astype(BF16))

    def inner_pair(i, carry):
        q = leaf_count - 2 - i
        both = children(q)
        paths[2 * q] = both[:, :rank]
        paths[2 * q + 1] = pltpu.roll(both, 64, 1)[:, :rank]

        @pl.when(i % 3 == 2)
        def _():
            pump(2 + i // 3)

        return carry

    lax.fori_loop(0, pairs - 1, inner_pair, 0)

    pumped = 2 + (pairs - 1) // 3

    def leaf_pairs(g, carry):
        for i in range(half):
            high, low = split(children(g * half + i))
            leaf_path[g * half + i] = jnp.concatenate([high, high, low], axis=1)
        pump(pumped + g)
        return carry

    lax.fori_loop(0, 2, leaf_pairs, 0)

    def accept(src, at_held, lo):
        both = src[:, lanes(lo)]
        held[at_held + 2 * lo] = both[:, :leaf_size]
        held[at_held + 2 * lo + 1] = both[:, leaf_size:]

    load_omega.wait()
    for i in range(pairs):
        accept(omega_v, leaf_count, i)
    up_acc[...] = jnp.zeros_like(up_acc)
    load_samples.wait()
    load_basis.wait()
    load_near.wait()

    lower = lax.broadcasted_iota(jnp.int32, (leaf_size, 128), 1) < 64
    base = leaf * leaf_count - leaf_count

    def near_product(p):
        tiles = []
        for k in range(slots):
            at = jnp.clip(index_ref[k, p] - base, 0, 3 * leaf_count - 1)
            live = jnp.where(k < count_ref[p], 1.0, 0.0)
            tiles.append(held[at] * jnp.full((1, leaf_size), live, F32).astype(BF16))
        blocks = jnp.concatenate([near_v[p, k] for k in range(slots)], axis=1)
        return dot_nt(jnp.concatenate(tiles, axis=1), blocks)

    def process(u, w):
        near = jnp.concatenate([near_product(2 * u), near_product(2 * u + 1)], axis=0)
        mine = samples_v[:, lanes(u)]
        mine = jnp.concatenate([mine[:, :leaf_size], mine[:, leaf_size:]], axis=0)
        far = (mine.astype(F32) - near).astype(BF16)
        basis = basis_v[pl.ds(2 * u, 2)].reshape(2 * rank, leaf_size)
        both = dot_nt(basis, far)
        top, bottom = both[:rank], both[rank:]
        coeff_v[2 * u] = top[:, :width]
        coeff_v[2 * u + 1] = pltpu.roll(bottom, 64, 1)[:, :width]
        low_lane = lower[:rank]
        top = jnp.where(low_lane, top, 0.0)
        bottom = jnp.where(low_lane, 0.0, bottom)
        top_high, top_low = split(top)
        bottom_high, bottom_low = split(bottom)
        block_high = jnp.concatenate([top_high, bottom_high], axis=0)
        block_low = jnp.concatenate([top_low, bottom_low], axis=0)
        row_high = top_high + bottom_high
        row_low = top_low + bottom_low
        gram = dot_nt(
            jnp.concatenate([row_high, row_high, row_low], axis=1),
            jnp.concatenate([block_high, block_low, block_high], axis=1),
        ) * (1.0 / total_columns)
        for t in range(n_samp):
            gram_send[t, pl.ds(pl.multiple_of(w * part, part), part), :] = (
                gram[t * part:(t + 1) * part].astype(gram_send.dtype)
            )
        return dot(leaf_path[u], jnp.concatenate([block_high, block_low, block_high], axis=0))

    def receive(c):
        @pl.when(leaf > 0)
        def _():
            to_right(c).wait_recv()
            accept(land_l, 0, pairs - 1 - c)

        @pl.when(leaf < n_leaf - 1)
        def _():
            to_left(c).wait_recv()
            accept(land_r, 2 * leaf_count, c)

    def first(c, carry):
        receive(c)
        return carry

    lax.fori_loop(0, half, first, 0)

    span = 2 * part

    def gram_copy(d, j):
        at = pl.ds(pl.multiple_of(j * span, span), span)
        return pltpu.make_async_remote_copy(
            src_ref=gram_send.at[samp ^ d, at], dst_ref=gram_recv.at[d - 1, at],
            send_sem=gram_ssem.at[d - 1, j], recv_sem=gram_rsem.at[d - 1, j],
            device_id=(leaf, samp ^ d), device_id_type=MESH,
        )

    def out_copy(j, side):
        at = pl.ds(2 * (half - 1 - j) if side == 0 else 2 * (half + j), 2)
        return pltpu.make_async_copy(coeff_v.at[at], coeff_hbm.at[at], out_sem.at[side, j])

    def step(j, carry):
        lo_l = half - 1 - j
        lo_r = half + j

        receive(half + j)
        up_acc[...] += process(lo_l, 2 * j) + process(lo_r, 2 * j + 1)
        for d in range(1, n_samp):
            gram_copy(d, j).start()
        out_copy(j, 0).start()
        out_copy(j, 1).start()

        @pl.when(j < steps - 1)
        def _():
            pump(half + 1 + j)

        return carry

    lax.fori_loop(0, steps, step, 0)

    total = up_acc[...]
    total_high, total_low = split(total + pltpu.roll(total, 64, 1))
    total = dot(ascend[...], jnp.concatenate([total_high, total_low, total_high], axis=0))
    side = rank // 2
    for h in range(heights):
        up_send[h * side:(h + 1) * side] = jnp.where(
            lower[:side], total[h * rank:h * rank + side], total[h * rank + side:(h + 1) * rank]
        )

    def up_copy(d):
        first = (d.bit_length() - 1) * side
        at = pl.ds(first, heights * side - first)
        return pltpu.make_async_remote_copy(
            src_ref=up_send.at[at], dst_ref=up_recv.at[d - 1, at],
            send_sem=up_ssem.at[d - 1], recv_sem=up_rsem.at[d - 1],
            device_id=(leaf ^ d, samp), device_id_type=MESH,
        )

    for d in range(1, n_leaf):
        up_copy(d).start()

    def gram_wait(j, carry):
        for d in range(1, n_samp):
            gram_copy(d, j).wait_recv()
        return carry

    lax.fori_loop(0, steps, gram_wait, 0)
    for w in range(pairs):
        u = half - 1 - w // 2 if w % 2 == 0 else half + w // 2
        at = slice(w * part, (w + 1) * part)
        value = gram_send[samp, at, :].astype(F32)
        for d in range(1, n_samp):
            value = value + gram_recv[d - 1, at, :].astype(F32)
        gram_sum[u * part:(u + 1) * part, :] = value
    low16 = lower[:pairs]
    for m in range(part // 2):
        first = gram_sum[pl.ds(2 * m, pairs, stride=part), :]
        second = gram_sum[pl.ds(2 * m + 1, pairs, stride=part), :]
        even = jnp.where(low16, first, pltpu.roll(second, 64, 1))
        odd = jnp.where(low16, pltpu.roll(first, 64, 1), second)
        lo = m * leaf_count
        gram_mix[pl.ds(lo, pairs, stride=2), :] = even
        gram_mix[pl.ds(lo + 1, pairs, stride=2), :] = odd
        gram_ref[:, 128 * m:128 * m + 128] = gram_mix[lo:lo + leaf_count, :]

    for d in range(1, n_leaf):
        up_copy(d).wait_recv()
    for h in range(heights):
        at = slice(h * side, (h + 1) * side)
        value = up_send[at, :]
        for d in range(1, n_leaf):
            if d.bit_length() <= h + 1:
                value = value + up_recv[d - 1, at, :]
        ancestor_ref[h, 0:side, :] = value[:, :width]
        ancestor_ref[h, side:rank, :] = pltpu.roll(value, 64, 1)[:, :width]

    def finish(j, carry):
        for d in range(1, n_samp):
            gram_copy(d, j).wait_send()
        out_copy(j, 0).wait()
        out_copy(j, 1).wait()
        return carry

    lax.fori_loop(0, steps, finish, 0)
    for d in range(1, n_leaf):
        up_copy(d).wait_send()


def deliver(count, *refs):
    sources, targets, rooms = refs[:count], refs[count:2 * count], refs[2 * count:3 * count]
    sems = refs[-1]
    reads = [pltpu.make_async_copy(sources[i], rooms[i], sems.at[0, i]) for i in range(count)]
    writes = [pltpu.make_async_copy(rooms[i], targets[i], sems.at[1, i]) for i in range(count)]
    for read in reads:
        read.start()
    for read, write in zip(reads, writes):
        read.wait()
        write.start()
    for write in writes:
        write.wait()


def shards(
    n_leaf, n_samp,
    samples, omega, leaf_basis, near_blocks, near_index, near_count, inner_transfer, upper_transfer
):
    leaf_count, rank, leaf_size = leaf_basis.shape
    width = samples.shape[1]
    pairs = leaf_count // 2
    steps = pairs // 2
    heights = n_leaf.bit_length() - 1
    part = rank // n_samp
    nodes = inner_transfer.shape[0]
    upper_nodes = upper_transfer.shape[0]
    wire = BF16 if part % 16 == 0 else F32
    omega, samples, near_index = omega.T, samples.T, near_index.T
    vmem = pl.BlockSpec(memory_space=pltpu.VMEM)
    smem = pl.BlockSpec(memory_space=pltpu.SMEM)
    hbm = pl.BlockSpec(memory_space=pl.ANY)
    dma = pltpu.SemaphoreType.DMA
    coeffs, gram, ancestors = pl.pallas_call(
        functools.partial(kernel, n_leaf, n_samp, width * n_samp),
        out_shape=(
            jax.ShapeDtypeStruct((leaf_count, rank, width), F32),
            jax.ShapeDtypeStruct((leaf_count, part * rank), F32),
            jax.ShapeDtypeStruct((heights, rank, width), F32),
        ),
        in_specs=[smem, smem, vmem, vmem, hbm, hbm, hbm, hbm],
        out_specs=(hbm, vmem, vmem),
        scratch_shapes=[
            pltpu.VMEM(omega.shape, BF16),
            pltpu.VMEM(samples.shape, BF16),
            pltpu.VMEM(leaf_basis.shape, BF16),
            pltpu.VMEM(near_blocks.shape, BF16),
            pltpu.VMEM(omega.shape, BF16),
            pltpu.VMEM(omega.shape, BF16),
            pltpu.VMEM((3 * leaf_count, width, leaf_size), BF16),
            pltpu.VMEM((nodes * rank, 128), F32),
            pltpu.VMEM((upper_nodes * rank, 128), F32),
            pltpu.VMEM((nodes + 1, rank, rank), F32),
            pltpu.VMEM((heights * rank, 3 * rank), BF16),
            pltpu.VMEM((pairs, rank, 384), BF16),
            pltpu.VMEM((rank, 128), F32),
            pltpu.VMEM((heights * rank // 2, 128), F32),
            pltpu.VMEM((n_leaf - 1, heights * rank // 2, 128), F32),
            pltpu.VMEM((n_samp, pairs * part, 128), wire),
            pltpu.VMEM((n_samp - 1, pairs * part, 128), wire),
            pltpu.VMEM((pairs * part, 128), F32),
            pltpu.VMEM((part // 2 * leaf_count, 128), F32),
            pltpu.VMEM((leaf_count, rank, width), F32),
            dma((3,)), dma,
            dma((pairs,)), dma((pairs,)), dma((pairs,)), dma((pairs,)),
            dma((n_samp - 1, steps)), dma((n_samp - 1, steps)),
            dma((n_leaf - 1,)), dma((n_leaf - 1,)),
            dma((2, steps)),
        ],
        compiler_params=pltpu.CompilerParams(
            collective_id=0, has_side_effects=True, vmem_limit_bytes=56 * 1024 * 1024
        ),
    )(near_index, near_count, inner_transfer, upper_transfer, omega, samples, leaf_basis, near_blocks)
    results = (coeffs, gram, ancestors[None])
    return pl.pallas_call(
        functools.partial(deliver, len(results)),
        out_shape=tuple(jax.ShapeDtypeStruct(x.shape, x.dtype) for x in results),
        in_specs=[hbm] * len(results),
        out_specs=(hbm,) * len(results),
        scratch_shapes=[pltpu.VMEM(x.shape, x.dtype) for x in results] + [dma((2, len(results)))],
        compiler_params=pltpu.CompilerParams(vmem_limit_bytes=62 * 1024 * 1024),
    )(*results)


def solution(mesh):
    return jax.shard_map(
        functools.partial(shards, mesh.shape["leaf"], mesh.shape["samp"]),
        mesh=mesh,
        in_specs=(
            P("leaf", "samp"),
            P("leaf", "samp"),
            P("leaf", None, None),
            P("leaf", None, None, None),
            P("leaf", None),
            P("leaf"),
            P("leaf", None),
            P(),
        ),
        out_specs=(P("leaf", None, "samp"), P("leaf", "samp"), P("leaf", None, None, "samp")),
        check_vma=False,
    )
```

```python
import functools

import jax
import jax.numpy as jnp
from jax import lax
from jax.experimental import pallas as pl
from jax.experimental.pallas import tpu as pltpu
from jax.sharding import PartitionSpec as P

MESH = pl.DeviceIdType.MESH
F32 = jnp.float32
BF16 = jnp.bfloat16


def split(x):
    high = x.astype(BF16)
    return high, (x - high.astype(F32)).astype(BF16)


def dot_nt(a, b):
    return lax.dot_general(a, b, (((1,), (1,)), ((), ())), preferred_element_type=F32)


def dot(a, b):
    return jnp.dot(a, b, preferred_element_type=F32)


def chain_step(rows, mats):
    high, low = split(rows)
    n = rows.shape[0]
    both = dot_nt(jnp.concatenate([high, low], axis=0), mats)
    return both[:n] + both[n:]


def kernel(
    n_leaf, n_samp, total_columns,
    index_ref, count_ref, inner_hbm, upper_hbm, omega_hbm, samples_hbm, basis_hbm, near_hbm,
    coeff_hbm, gram_ref, ancestor_ref,
    inner_ref, upper_ref, omega_v, samples_v, basis_v, near_v, land_l, land_r, held,
    inner_v, upper_v, paths, ascend, leaf_path, up_acc, up_send, up_recv,
    gram_send, gram_recv, gram_sum, gram_mix, coeff_v, far_v,
    load_sem, near_sem, send_l, send_r, recv_l, recv_r,
    gram_ssem, gram_rsem, up_ssem, up_rsem, out_sem,
):
    leaf = lax.axis_index("leaf")
    samp = lax.axis_index("samp")
    leaf_count, rank, leaf_size = basis_v.shape
    slots = near_v.shape[1]
    width = omega_v.shape[0]
    pairs = leaf_count // 2
    half = pairs // 2
    heights = ancestor_ref.shape[0]
    steps = half
    part = rank // n_samp
    nodes = inner_ref.shape[0]

    load_omega = pltpu.make_async_copy(omega_hbm, omega_v, load_sem.at[0])
    load_samples = pltpu.make_async_copy(samples_hbm, samples_v, load_sem.at[1])
    load_basis = pltpu.make_async_copy(basis_hbm, basis_v, load_sem.at[2])
    load_near = pltpu.make_async_copy(near_hbm, near_v, near_sem)
    load_inner = pltpu.make_async_copy(inner_hbm, inner_ref, load_sem.at[3])
    load_upper = pltpu.make_async_copy(upper_hbm, upper_ref, load_sem.at[4])
    load_inner.start()
    load_upper.start()
    load_omega.start()
    load_samples.start()
    load_basis.start()
    load_near.start()

    barrier = pltpu.get_barrier_semaphore()
    for d in range(1, n_leaf):
        pl.semaphore_signal(barrier, inc=1, device_id=(leaf ^ d, samp), device_id_type=MESH)
    for d in range(1, n_samp):
        pl.semaphore_signal(barrier, inc=1, device_id=(leaf, samp ^ d), device_id_type=MESH)

    pl.semaphore_wait(barrier, n_leaf + n_samp - 2)

    def lanes(pair):
        unit = 2 * leaf_size
        return pl.ds(pl.multiple_of(pair * unit, unit), unit)

    def to_right(c):
        at = lanes(pairs - 1 - c)
        return pltpu.make_async_remote_copy(
            src_ref=omega_hbm.at[:, at], dst_ref=land_l.at[:, at],
            send_sem=send_r.at[c], recv_sem=recv_l.at[c],
            device_id=(leaf + 1, samp), device_id_type=MESH,
        )

    def to_left(c):
        at = lanes(c)
        return pltpu.make_async_remote_copy(
            src_ref=omega_hbm.at[:, at], dst_ref=land_r.at[:, at],
            send_sem=send_l.at[c], recv_sem=recv_r.at[c],
            device_id=(leaf - 1, samp), device_id_type=MESH,
        )

    def send(c):
        @pl.when(leaf < n_leaf - 1)
        def _():
            to_right(c).start()

        @pl.when(leaf > 0)
        def _():
            to_left(c).start()

    window = 4

    def pump(c):
        @pl.when(leaf < n_leaf - 1)
        def _():
            to_right(c).wait_send()

        @pl.when(leaf > 0)
        def _():
            to_left(c).wait_send()

        @pl.when(c + window < pairs)
        def _():
            send(c + window)

    for c in range(window):
        send(c)

    load_inner.wait()
    load_upper.wait()
    lines = rank * rank // 128
    for r in range(lines):
        if r % (lines // 2) == 0 and r > 0:
            pump(r // (lines // 2) - 1)
        for src, dst in ((inner_ref, inner_v), (upper_ref, upper_v)):
            count = src.shape[0]
            tile = src[:, 128 * r:128 * r + 128].astype(F32)
            dst[pl.ds(2 * r, count, stride=rank), :] = tile
            dst[pl.ds(2 * r + 1, count, stride=rank), :] = pltpu.roll(tile, 64, 1)

    pump(1)

    eye = (
        lax.broadcasted_iota(jnp.int32, (rank, rank), 0)
        == lax.broadcasted_iota(jnp.int32, (rank, rank), 1)
    ).astype(F32)
    rows = None
    starts = []
    offset = 0
    for h in range(heights):
        starts.append(offset)
        offset += n_leaf >> h
    for h in reversed(range(heights)):
        node = starts[h] + lax.shift_right_logical(leaf, h)
        mat = upper_v[pl.ds(pl.multiple_of(node * rank, rank), rank), :][:, :rank].astype(BF16)
        rows = eye if rows is None else jnp.concatenate([eye, rows], axis=0)
        rows = chain_step(rows, mat)
    rows_high, rows_low = split(rows)
    ascend[...] = jnp.concatenate([rows_high, rows_high, rows_low], axis=1)
    paths[nodes] = eye

    def children(q):
        mats = inner_v[pl.ds(pl.multiple_of(q * 2 * rank, 2 * rank), 2 * rank), :]
        return chain_step(paths[leaf_count + q], mats[:, :rank].astype(BF16))

    def inner_pair(i, carry):
        q = leaf_count - 2 - i
        both = children(q)
        paths[2 * q] = both[:, :rank]
        paths[2 * q + 1] = pltpu.roll(both, 64, 1)[:, :rank]

        @pl.when(i % 3 == 2)
        def _():
            pump(2 + i // 3)

        return carry

    lax.fori_loop(0, pairs - 1, inner_pair, 0)

    pumped = 2 + (pairs - 1) // 3

    def leaf_pairs(g, carry):
        for i in range(half):
            high, low = split(children(g * half + i))
            leaf_path[g * half + i] = jnp.concatenate([high, high, low], axis=1)
        pump(pumped + g)
        return carry

    lax.fori_loop(0, 2, leaf_pairs, 0)

    def accept(src, at_held, lo):
        both = src[:, lanes(lo)]
        held[at_held + 2 * lo] = both[:, :leaf_size]
        held[at_held + 2 * lo + 1] = both[:, leaf_size:]

    load_omega.wait()
    for i in range(pairs):
        accept(omega_v, leaf_count, i)
    up_acc[...] = jnp.zeros_like(up_acc)
    load_samples.wait()
    load_basis.wait()
    load_near.wait()

    lower = lax.broadcasted_iota(jnp.int32, (leaf_size, 128), 1) < 64
    base = leaf * leaf_count - leaf_count

    def near_product(p):
        tiles = []
        for k in range(slots):
            at = jnp.clip(index_ref[k, p] - base, 0, 3 * leaf_count - 1)
            live = jnp.where(k < count_ref[p], 1.0, 0.0)
            tiles.append(held[at] * jnp.full((1, leaf_size), live, F32).astype(BF16))
        blocks = jnp.concatenate([near_v[p, k] for k in range(slots)], axis=1)
        return dot_nt(jnp.concatenate(tiles, axis=1), blocks)

    def near_stage(u, w):
        near = jnp.concatenate([near_product(2 * u), near_product(2 * u + 1)], axis=0)
        mine = samples_v[:, lanes(u)]
        mine = jnp.concatenate([mine[:, :leaf_size], mine[:, leaf_size:]], axis=0)
        far_v[w] = (mine.astype(F32) - near).astype(BF16)

    def post_stage(u, w):
        far = far_v[w]
        basis = basis_v[pl.ds(2 * u, 2)].reshape(2 * rank, leaf_size)
        both = dot_nt(basis, far)
        top, bottom = both[:rank], both[rank:]
        coeff_v[2 * u] = top[:, :width]
        coeff_v[2 * u + 1] = pltpu.roll(bottom, 64, 1)[:, :width]
        low_lane = lower[:rank]
        top = jnp.where(low_lane, top, 0.0)
        bottom = jnp.where(low_lane, 0.0, bottom)
        top_high, top_low = split(top)
        bottom_high, bottom_low = split(bottom)
        block_high = jnp.concatenate([top_high, bottom_high], axis=0)
        block_low = jnp.concatenate([top_low, bottom_low], axis=0)
        row_high = top_high + bottom_high
        row_low = top_low + bottom_low
        gram = dot_nt(
            jnp.concatenate([row_high, row_high, row_low], axis=1),
            jnp.concatenate([block_high, block_low, block_high], axis=1),
        ) * (1.0 / total_columns)
        for t in range(n_samp):
            gram_send[t, pl.ds(pl.multiple_of(w * part, part), part), :] = (
                gram[t * part:(t + 1) * part].astype(gram_send.dtype)
            )
        return dot(leaf_path[u], jnp.concatenate([block_high, block_low, block_high], axis=0))

    def receive(c):
        @pl.when(leaf > 0)
        def _():
            to_right(c).wait_recv()
            accept(land_l, 0, pairs - 1 - c)

        @pl.when(leaf < n_leaf - 1)
        def _():
            to_left(c).wait_recv()
            accept(land_r, 2 * leaf_count, c)

    def first(c, carry):
        receive(c)
        return carry

    lax.fori_loop(0, half, first, 0)

    span = 4 * part

    def gram_copy(d, j):
        at = pl.ds(pl.multiple_of(j * span, span), span)
        return pltpu.make_async_remote_copy(
            src_ref=gram_send.at[samp ^ d, at], dst_ref=gram_recv.at[d - 1, at],
            send_sem=gram_ssem.at[d - 1, j], recv_sem=gram_rsem.at[d - 1, j],
            device_id=(leaf, samp ^ d), device_id_type=MESH,
        )

    quarter = leaf_count // 4

    def out_copy(i):
        at = pl.ds((quarter, 0, 3 * quarter)[i], (2 * quarter, quarter, quarter)[i])
        return pltpu.make_async_copy(coeff_v.at[at], coeff_hbm.at[at], out_sem.at[i])

    def nears(j):
        near_stage(half - 1 - j, 2 * j)
        near_stage(half + j, 2 * j + 1)

    def posts(j):
        up_acc[...] += post_stage(half - 1 - j, 2 * j) + post_stage(half + j, 2 * j + 1)

    receive(half)
    nears(0)
    pump(half + 1)

    def step(j, carry):
        receive(half + j)
        posts(j - 1)
        nears(j)

        @pl.when(j % 2 == 0)
        def _():
            for d in range(1, n_samp):
                gram_copy(d, j // 2 - 1).start()

        @pl.when(j < steps - 1)
        def _():
            pump(half + 1 + j)

        @pl.when(j == steps // 2)
        def _():
            out_copy(0).start()

        return carry

    lax.fori_loop(1, steps, step, 0)
    posts(steps - 1)
    for d in range(1, n_samp):
        gram_copy(d, steps // 2 - 1).start()

    total = up_acc[...]
    total_high, total_low = split(total + pltpu.roll(total, 64, 1))
    total = dot(ascend[...], jnp.concatenate([total_high, total_low, total_high], axis=0))
    side = rank // 2
    for h in range(heights):
        up_send[h * side:(h + 1) * side] = jnp.where(
            lower[:side], total[h * rank:h * rank + side], total[h * rank + side:(h + 1) * rank]
        )

    def up_copy(d):
        first = (d.bit_length() - 1) * side
        at = pl.ds(first, heights * side - first)
        return pltpu.make_async_remote_copy(
            src_ref=up_send.at[at], dst_ref=up_recv.at[d - 1, at],
            send_sem=up_ssem.at[d - 1], recv_sem=up_rsem.at[d - 1],
            device_id=(leaf ^ d, samp), device_id_type=MESH,
        )

    for d in range(1, n_leaf):
        up_copy(d).start()
    out_copy(1).start()
    out_copy(2).start()

    def gram_wait(j, carry):
        for d in range(1, n_samp):
            gram_copy(d, j).wait_recv()
        return carry

    lax.fori_loop(0, steps // 2, gram_wait, 0)
    for w in range(pairs):
        u = half - 1 - w // 2 if w % 2 == 0 else half + w // 2
        at = slice(w * part, (w + 1) * part)
        value = gram_send[samp, at, :].astype(F32)
        for d in range(1, n_samp):
            value = value + gram_recv[d - 1, at, :].astype(F32)
        gram_sum[u * part:(u + 1) * part, :] = value
    low16 = lower[:pairs]
    for m in range(part // 2):
        first = gram_sum[pl.ds(2 * m, pairs, stride=part), :]
        second = gram_sum[pl.ds(2 * m + 1, pairs, stride=part), :]
        even = jnp.where(low16, first, pltpu.roll(second, 64, 1))
        odd = jnp.where(low16, pltpu.roll(first, 64, 1), second)
        lo = m * leaf_count
        gram_mix[pl.ds(lo, pairs, stride=2), :] = even
        gram_mix[pl.ds(lo + 1, pairs, stride=2), :] = odd
        gram_ref[:, 128 * m:128 * m + 128] = gram_mix[lo:lo + leaf_count, :]

    for d in range(1, n_leaf):
        up_copy(d).wait_recv()
    for h in range(heights):
        at = slice(h * side, (h + 1) * side)
        value = up_send[at, :]
        for d in range(1, n_leaf):
            if d.bit_length() <= h + 1:
                value = value + up_recv[d - 1, at, :]
        ancestor_ref[h, 0:side, :] = value[:, :width]
        ancestor_ref[h, side:rank, :] = pltpu.roll(value, 64, 1)[:, :width]

    def finish(j, carry):
        for d in range(1, n_samp):
            gram_copy(d, j).wait_send()
        return carry

    lax.fori_loop(0, steps // 2, finish, 0)
    for i in range(3):
        out_copy(i).wait()
    for d in range(1, n_leaf):
        up_copy(d).wait_send()


def deliver(count, *refs):
    sources, targets, rooms = refs[:count], refs[count:2 * count], refs[2 * count:3 * count]
    sems = refs[-1]
    reads = [pltpu.make_async_copy(sources[i], rooms[i], sems.at[0, i]) for i in range(count)]
    writes = [pltpu.make_async_copy(rooms[i], targets[i], sems.at[1, i]) for i in range(count)]
    for read in reads:
        read.start()
    for read, write in zip(reads, writes):
        read.wait()
        write.start()
    for write in writes:
        write.wait()


def shards(
    n_leaf, n_samp,
    samples, omega, leaf_basis, near_blocks, near_index, near_count, inner_transfer, upper_transfer
):
    leaf_count, rank, leaf_size = leaf_basis.shape
    width = samples.shape[1]
    pairs = leaf_count // 2
    steps = pairs // 2
    heights = n_leaf.bit_length() - 1
    part = rank // n_samp
    nodes = inner_transfer.shape[0]
    upper_nodes = upper_transfer.shape[0]
    wire = BF16 if part % 16 == 0 else F32
    omega, samples, near_index = omega.T, samples.T, near_index.T
    vmem = pl.BlockSpec(memory_space=pltpu.VMEM)
    smem = pl.BlockSpec(memory_space=pltpu.SMEM)
    hbm = pl.BlockSpec(memory_space=pl.ANY)
    dma = pltpu.SemaphoreType.DMA
    coeffs, gram, ancestors = pl.pallas_call(
        functools.partial(kernel, n_leaf, n_samp, width * n_samp),
        out_shape=(
            jax.ShapeDtypeStruct((leaf_count, rank, width), F32),
            jax.ShapeDtypeStruct((leaf_count, part * rank), F32),
            jax.ShapeDtypeStruct((heights, rank, width), F32),
        ),
        in_specs=[smem, smem, hbm, hbm, hbm, hbm, hbm, hbm],
        out_specs=(hbm, vmem, vmem),
        scratch_shapes=[
            pltpu.VMEM(inner_transfer.shape, BF16),
            pltpu.VMEM(upper_transfer.shape, BF16),
            pltpu.VMEM(omega.shape, BF16),
            pltpu.VMEM(samples.shape, BF16),
            pltpu.VMEM(leaf_basis.shape, BF16),
            pltpu.VMEM(near_blocks.shape, BF16),
            pltpu.VMEM(omega.shape, BF16),
            pltpu.VMEM(omega.shape, BF16),
            pltpu.VMEM((3 * leaf_count, width, leaf_size), BF16),
            pltpu.VMEM((nodes * rank, 128), F32),
            pltpu.VMEM((upper_nodes * rank, 128), F32),
            pltpu.VMEM((nodes + 1, rank, rank), F32),
            pltpu.VMEM((heights * rank, 3 * rank), BF16),
            pltpu.VMEM((pairs, rank, 384), BF16),
            pltpu.VMEM((rank, 128), F32),
            pltpu.VMEM((heights * rank // 2, 128), F32),
            pltpu.VMEM((n_leaf - 1, heights * rank // 2, 128), F32),
            pltpu.VMEM((n_samp, pairs * part, 128), wire),
            pltpu.VMEM((n_samp - 1, pairs * part, 128), wire),
            pltpu.VMEM((pairs * part, 128), F32),
            pltpu.VMEM((part // 2 * leaf_count, 128), F32),
            pltpu.VMEM((leaf_count, rank, width), F32),
            pltpu.VMEM((pairs, leaf_size, leaf_size), BF16),
            dma((5,)), dma,
            dma((pairs,)), dma((pairs,)), dma((pairs,)), dma((pairs,)),
            dma((n_samp - 1, steps // 2)), dma((n_samp - 1, steps // 2)),
            dma((n_leaf - 1,)), dma((n_leaf - 1,)),
            dma((3,)),
        ],
        compiler_params=pltpu.CompilerParams(
            collective_id=0, has_side_effects=True, vmem_limit_bytes=56 * 1024 * 1024
        ),
    )(near_index, near_count, inner_transfer, upper_transfer, omega, samples, leaf_basis, near_blocks)
    results = (coeffs, gram, ancestors[None])
    return pl.pallas_call(
        functools.partial(deliver, len(results)),
        out_shape=tuple(jax.ShapeDtypeStruct(x.shape, x.dtype) for x in results),
        in_specs=[hbm] * len(results),
        out_specs=(hbm,) * len(results),
        scratch_shapes=[pltpu.VMEM(x.shape, x.dtype) for x in results] + [dma((2, len(results)))],
        compiler_params=pltpu.CompilerParams(vmem_limit_bytes=62 * 1024 * 1024),
    )(*results)


def solution(mesh):
    return jax.shard_map(
        functools.partial(shards, mesh.shape["leaf"], mesh.shape["samp"]),
        mesh=mesh,
        in_specs=(
            P("leaf", "samp"),
            P("leaf", "samp"),
            P("leaf", None, None),
            P("leaf", None, None, None),
            P("leaf", None),
            P("leaf"),
            P("leaf", None),
            P(),
        ),
        out_specs=(P("leaf", None, "samp"), P("leaf", "samp"), P("leaf", None, None, "samp")),
        check_vma=False,
    )
```

```python
import functools

import jax
import jax.numpy as jnp
from jax import lax
from jax.experimental import pallas as pl
from jax.experimental.pallas import tpu as pltpu
from jax.sharding import PartitionSpec as P

MESH = pl.DeviceIdType.MESH
F32 = jnp.float32
BF16 = jnp.bfloat16


def split(x):
    high = x.astype(BF16)
    return high, (x - high.astype(F32)).astype(BF16)


def dot_nt(a, b):
    return lax.dot_general(a, b, (((1,), (1,)), ((), ())), preferred_element_type=F32)


def dot(a, b):
    return jnp.dot(a, b, preferred_element_type=F32)


def chain_step(rows, mats):
    high, low = split(rows)
    n = rows.shape[0]
    both = dot_nt(jnp.concatenate([high, low], axis=0), mats)
    return both[:n] + both[n:]


def kernel(
    n_leaf, n_samp, total_columns,
    index_ref, count_ref, inner_hbm, upper_hbm, omega_hbm, samples_hbm, basis_hbm, near_hbm,
    coeff_hbm, gram_ref, ancestor_ref,
    inner_ref, upper_ref, omega_v, samples_v, basis_v, near_v, land_l, land_r, held,
    inner_v, upper_v, paths, ascend, leaf_path, up_acc, up_send, up_recv,
    gram_send, gram_recv, gram_sum, gram_mix, coeff_v, far_v,
    load_sem, near_sem, send_l, send_r, recv_l, recv_r,
    gram_ssem, gram_rsem, up_ssem, up_rsem, out_sem,
):
    leaf = lax.axis_index("leaf")
    samp = lax.axis_index("samp")
    leaf_count, rank, leaf_size = basis_v.shape
    slots = near_v.shape[1]
    width = omega_v.shape[0]
    pairs = leaf_count // 2
    half = pairs // 2
    heights = ancestor_ref.shape[0]
    steps = half
    part = rank // n_samp
    nodes = inner_ref.shape[0]

    load_omega = pltpu.make_async_copy(omega_hbm, omega_v, load_sem.at[0])
    load_samples = pltpu.make_async_copy(samples_hbm, samples_v, load_sem.at[1])
    load_basis = pltpu.make_async_copy(basis_hbm, basis_v, load_sem.at[2])
    load_near = pltpu.make_async_copy(near_hbm, near_v, near_sem)
    load_inner = pltpu.make_async_copy(inner_hbm, inner_ref, load_sem.at[3])
    load_upper = pltpu.make_async_copy(upper_hbm, upper_ref, load_sem.at[4])
    load_inner.start()
    load_upper.start()
    load_omega.start()
    load_samples.start()
    load_basis.start()
    load_near.start()

    barrier = pltpu.get_barrier_semaphore()
    for d in range(1, n_leaf):
        pl.semaphore_signal(barrier, inc=1, device_id=(leaf ^ d, samp), device_id_type=MESH)
    for d in range(1, n_samp):
        pl.semaphore_signal(barrier, inc=1, device_id=(leaf, samp ^ d), device_id_type=MESH)

    pl.semaphore_wait(barrier, n_leaf + n_samp - 2)

    def lanes(pair):
        unit = 2 * leaf_size
        return pl.ds(pl.multiple_of(pair * unit, unit), unit)

    def to_right(c):
        at = lanes(pairs - 1 - c)
        return pltpu.make_async_remote_copy(
            src_ref=omega_hbm.at[:, at], dst_ref=land_l.at[:, at],
            send_sem=send_r.at[c], recv_sem=recv_l.at[c],
            device_id=(leaf + 1, samp), device_id_type=MESH,
        )

    def to_left(c):
        at = lanes(c)
        return pltpu.make_async_remote_copy(
            src_ref=omega_hbm.at[:, at], dst_ref=land_r.at[:, at],
            send_sem=send_l.at[c], recv_sem=recv_r.at[c],
            device_id=(leaf - 1, samp), device_id_type=MESH,
        )

    def send(c):
        @pl.when(leaf < n_leaf - 1)
        def _():
            to_right(c).start()

        @pl.when(leaf > 0)
        def _():
            to_left(c).start()

    for c in range(half + 1):
        send(c)

    load_inner.wait()
    load_upper.wait()
    lines = rank * rank // 128
    for r in range(lines):
        for src, dst in ((inner_ref, inner_v), (upper_ref, upper_v)):
            count = src.shape[0]
            tile = src[:, 128 * r:128 * r + 128].astype(F32)
            dst[pl.ds(2 * r, count, stride=rank), :] = tile
            dst[pl.ds(2 * r + 1, count, stride=rank), :] = pltpu.roll(tile, 64, 1)

    eye = (
        lax.broadcasted_iota(jnp.int32, (rank, rank), 0)
        == lax.broadcasted_iota(jnp.int32, (rank, rank), 1)
    ).astype(F32)
    rows = None
    starts = []
    offset = 0
    for h in range(heights):
        starts.append(offset)
        offset += n_leaf >> h
    for h in reversed(range(heights)):
        node = starts[h] + lax.shift_right_logical(leaf, h)
        mat = upper_v[pl.ds(pl.multiple_of(node * rank, rank), rank), :][:, :rank].astype(BF16)
        rows = eye if rows is None else jnp.concatenate([eye, rows], axis=0)
        rows = chain_step(rows, mat)
    rows_high, rows_low = split(rows)
    ascend[...] = jnp.concatenate([rows_high, rows_high, rows_low], axis=1)
    paths[nodes] = eye

    for q in reversed(range(leaf_count - 1)):
        mats = inner_v[q * 2 * rank:(q + 1) * 2 * rank, :]
        both = chain_step(paths[leaf_count + q], mats[:, :rank].astype(BF16))
        if q < pairs:
            high, low = split(both)
            leaf_path[q] = jnp.concatenate([high, high, low], axis=1)
        else:
            paths[2 * q] = both[:, :rank]
            paths[2 * q + 1] = pltpu.roll(both, 64, 1)[:, :rank]

    def accept(src, at_held, lo):
        both = src[:, lanes(lo)]
        held[at_held + 2 * lo] = both[:, :leaf_size]
        held[at_held + 2 * lo + 1] = both[:, leaf_size:]

    load_omega.wait()
    for i in range(pairs):
        accept(omega_v, leaf_count, i)
    up_acc[...] = jnp.zeros_like(up_acc)
    load_samples.wait()
    load_basis.wait()
    load_near.wait()

    lower = lax.broadcasted_iota(jnp.int32, (leaf_size, 128), 1) < 64
    base = leaf * leaf_count - leaf_count

    def near_product(p):
        tiles = []
        for k in range(slots):
            at = jnp.clip(index_ref[k, p] - base, 0, 3 * leaf_count - 1)
            live = jnp.where(k < count_ref[p], 1.0, 0.0)
            tiles.append(held[at] * jnp.full((1, leaf_size), live, F32).astype(BF16))
        blocks = jnp.concatenate([near_v[p, k] for k in range(slots)], axis=1)
        return dot_nt(jnp.concatenate(tiles, axis=1), blocks)

    def near_stage(u, w):
        near = jnp.concatenate([near_product(2 * u), near_product(2 * u + 1)], axis=0)
        mine = samples_v[:, lanes(u)]
        mine = jnp.concatenate([mine[:, :leaf_size], mine[:, leaf_size:]], axis=0)
        far_v[w] = (mine.astype(F32) - near).astype(BF16)

    def post_stage(u, w):
        far = far_v[w]
        basis = basis_v[pl.ds(2 * u, 2)].reshape(2 * rank, leaf_size)
        both = dot_nt(basis, far)
        top, bottom = both[:rank], both[rank:]
        coeff_v[2 * u] = top[:, :width]
        coeff_v[2 * u + 1] = pltpu.roll(bottom, 64, 1)[:, :width]
        low_lane = lower[:rank]
        top = jnp.where(low_lane, top, 0.0)
        bottom = jnp.where(low_lane, 0.0, bottom)
        top_high, top_low = split(top)
        bottom_high, bottom_low = split(bottom)
        block_high = jnp.concatenate([top_high, bottom_high], axis=0)
        block_low = jnp.concatenate([top_low, bottom_low], axis=0)
        row_high = top_high + bottom_high
        row_low = top_low + bottom_low
        gram = dot_nt(
            jnp.concatenate([row_high, row_high, row_low], axis=1),
            jnp.concatenate([block_high, block_low, block_high], axis=1),
        ) * (1.0 / total_columns)
        for t in range(n_samp):
            gram_send[t, pl.ds(pl.multiple_of(w * part, part), part), :] = (
                gram[t * part:(t + 1) * part].astype(gram_send.dtype)
            )
        return dot(leaf_path[u], jnp.concatenate([block_high, block_low, block_high], axis=0))

    def receive(c):
        @pl.when(leaf > 0)
        def _():
            to_right(c).wait_recv()
            accept(land_l, 0, pairs - 1 - c)

        @pl.when(leaf < n_leaf - 1)
        def _():
            to_left(c).wait_recv()
            accept(land_r, 2 * leaf_count, c)

    send(half + 1)
    for c in range(half):
        receive(c)
        if c == half // 2:
            send(half + 2)
    send(half + 3)

    span = 4 * part

    def gram_copy(d, j):
        at = pl.ds(pl.multiple_of(j * span, span), span)
        return pltpu.make_async_remote_copy(
            src_ref=gram_send.at[samp ^ d, at], dst_ref=gram_recv.at[d - 1, at],
            send_sem=gram_ssem.at[d - 1, j], recv_sem=gram_rsem.at[d - 1, j],
            device_id=(leaf, samp ^ d), device_id_type=MESH,
        )

    quarter = leaf_count // 4

    def out_copy(i):
        at = pl.ds((quarter, 0, 3 * quarter)[i], (2 * quarter, quarter, quarter)[i])
        return pltpu.make_async_copy(coeff_v.at[at], coeff_hbm.at[at], out_sem.at[i])

    def nears(j):
        near_stage(half - 1 - j, 2 * j)
        near_stage(half + j, 2 * j + 1)

    def posts(j):
        up_acc[...] += post_stage(half - 1 - j, 2 * j) + post_stage(half + j, 2 * j + 1)

    receive(half)
    send(half + 4)
    nears(0)

    def step(j, carry):
        receive(half + j)

        @pl.when(half + 4 + j < pairs)
        def _():
            send(half + 4 + j)

        posts(j - 1)
        nears(j)

        @pl.when(j % 2 == 0)
        def _():
            for d in range(1, n_samp):
                gram_copy(d, j // 2 - 1).start()

        @pl.when(j == steps // 2)
        def _():
            out_copy(0).start()

        return carry

    lax.fori_loop(1, steps, step, 0)
    posts(steps - 1)
    for d in range(1, n_samp):
        gram_copy(d, steps // 2 - 1).start()

    total = up_acc[...]
    total_high, total_low = split(total + pltpu.roll(total, 64, 1))
    total = dot(ascend[...], jnp.concatenate([total_high, total_low, total_high], axis=0))
    side = rank // 2
    for h in range(heights):
        up_send[h * side:(h + 1) * side] = jnp.where(
            lower[:side], total[h * rank:h * rank + side], total[h * rank + side:(h + 1) * rank]
        )

    def up_copy(d):
        first = (d.bit_length() - 1) * side
        at = pl.ds(first, heights * side - first)
        return pltpu.make_async_remote_copy(
            src_ref=up_send.at[at], dst_ref=up_recv.at[d - 1, at],
            send_sem=up_ssem.at[d - 1], recv_sem=up_rsem.at[d - 1],
            device_id=(leaf ^ d, samp), device_id_type=MESH,
        )

    for d in range(1, n_leaf):
        up_copy(d).start()
    out_copy(1).start()
    out_copy(2).start()

    def gram_wait(j, carry):
        for d in range(1, n_samp):
            gram_copy(d, j).wait_recv()
        return carry

    lax.fori_loop(0, steps // 2, gram_wait, 0)
    for w in range(pairs):
        u = half - 1 - w // 2 if w % 2 == 0 else half + w // 2
        at = slice(w * part, (w + 1) * part)
        value = gram_send[samp, at, :].astype(F32)
        for d in range(1, n_samp):
            value = value + gram_recv[d - 1, at, :].astype(F32)
        gram_sum[u * part:(u + 1) * part, :] = value
    low16 = lower[:pairs]
    for m in range(part // 2):
        first = gram_sum[pl.ds(2 * m, pairs, stride=part), :]
        second = gram_sum[pl.ds(2 * m + 1, pairs, stride=part), :]
        even = jnp.where(low16, first, pltpu.roll(second, 64, 1))
        odd = jnp.where(low16, pltpu.roll(first, 64, 1), second)
        lo = m * leaf_count
        gram_mix[pl.ds(lo, pairs, stride=2), :] = even
        gram_mix[pl.ds(lo + 1, pairs, stride=2), :] = odd
        gram_ref[:, 128 * m:128 * m + 128] = gram_mix[lo:lo + leaf_count, :]

    for d in range(1, n_leaf):
        up_copy(d).wait_recv()
    for h in range(heights):
        at = slice(h * side, (h + 1) * side)
        value = up_send[at, :]
        for d in range(1, n_leaf):
            if d.bit_length() <= h + 1:
                value = value + up_recv[d - 1, at, :]
        ancestor_ref[h, 0:side, :] = value[:, :width]
        ancestor_ref[h, side:rank, :] = pltpu.roll(value, 64, 1)[:, :width]

    def finish(j, carry):
        for d in range(1, n_samp):
            gram_copy(d, j).wait_send()
        return carry

    lax.fori_loop(0, steps // 2, finish, 0)

    def sent(c, carry):
        @pl.when(leaf < n_leaf - 1)
        def _():
            to_right(c).wait_send()

        @pl.when(leaf > 0)
        def _():
            to_left(c).wait_send()

        return carry

    lax.fori_loop(0, pairs, sent, 0)
    for i in range(3):
        out_copy(i).wait()
    for d in range(1, n_leaf):
        up_copy(d).wait_send()


def deliver(count, *refs):
    sources, targets, rooms = refs[:count], refs[count:2 * count], refs[2 * count:3 * count]
    sems = refs[-1]
    reads = [pltpu.make_async_copy(sources[i], rooms[i], sems.at[0, i]) for i in range(count)]
    writes = [pltpu.make_async_copy(rooms[i], targets[i], sems.at[1, i]) for i in range(count)]
    for read in reads:
        read.start()
    for read, write in zip(reads, writes):
        read.wait()
        write.start()
    for write in writes:
        write.wait()


def shards(
    n_leaf, n_samp,
    samples, omega, leaf_basis, near_blocks, near_index, near_count, inner_transfer, upper_transfer
):
    leaf_count, rank, leaf_size = leaf_basis.shape
    width = samples.shape[1]
    pairs = leaf_count // 2
    steps = pairs // 2
    heights = n_leaf.bit_length() - 1
    part = rank // n_samp
    nodes = inner_transfer.shape[0]
    upper_nodes = upper_transfer.shape[0]
    wire = BF16 if part % 16 == 0 else F32
    omega, samples, near_index = omega.T, samples.T, near_index.T
    vmem = pl.BlockSpec(memory_space=pltpu.VMEM)
    smem = pl.BlockSpec(memory_space=pltpu.SMEM)
    hbm = pl.BlockSpec(memory_space=pl.ANY)
    dma = pltpu.SemaphoreType.DMA
    coeffs, gram, ancestors = pl.pallas_call(
        functools.partial(kernel, n_leaf, n_samp, width * n_samp),
        out_shape=(
            jax.ShapeDtypeStruct((leaf_count, rank, width), F32),
            jax.ShapeDtypeStruct((leaf_count, part * rank), F32),
            jax.ShapeDtypeStruct((heights, rank, width), F32),
        ),
        in_specs=[smem, smem, hbm, hbm, hbm, hbm, hbm, hbm],
        out_specs=(hbm, vmem, vmem),
        scratch_shapes=[
            pltpu.VMEM(inner_transfer.shape, BF16),
            pltpu.VMEM(upper_transfer.shape, BF16),
            pltpu.VMEM(omega.shape, BF16),
            pltpu.VMEM(samples.shape, BF16),
            pltpu.VMEM(leaf_basis.shape, BF16),
            pltpu.VMEM(near_blocks.shape, BF16),
            pltpu.VMEM(omega.shape, BF16),
            pltpu.VMEM(omega.shape, BF16),
            pltpu.VMEM((3 * leaf_count, width, leaf_size), BF16),
            pltpu.VMEM((nodes * rank, 128), F32),
            pltpu.VMEM((upper_nodes * rank, 128), F32),
            pltpu.VMEM((nodes + 1, rank, rank), F32),
            pltpu.VMEM((heights * rank, 3 * rank), BF16),
            pltpu.VMEM((pairs, rank, 384), BF16),
            pltpu.VMEM((rank, 128), F32),
            pltpu.VMEM((heights * rank // 2, 128), F32),
            pltpu.VMEM((n_leaf - 1, heights * rank // 2, 128), F32),
            pltpu.VMEM((n_samp, pairs * part, 128), wire),
            pltpu.VMEM((n_samp - 1, pairs * part, 128), wire),
            pltpu.VMEM((pairs * part, 128), F32),
            pltpu.VMEM((part // 2 * leaf_count, 128), F32),
            pltpu.VMEM((leaf_count, rank, width), F32),
            pltpu.VMEM((pairs, leaf_size, leaf_size), BF16),
            dma((5,)), dma,
            dma((pairs,)), dma((pairs,)), dma((pairs,)), dma((pairs,)),
            dma((n_samp - 1, steps // 2)), dma((n_samp - 1, steps // 2)),
            dma((n_leaf - 1,)), dma((n_leaf - 1,)),
            dma((3,)),
        ],
        compiler_params=pltpu.CompilerParams(
            collective_id=0, has_side_effects=True, vmem_limit_bytes=56 * 1024 * 1024
        ),
    )(near_index, near_count, inner_transfer, upper_transfer, omega, samples, leaf_basis, near_blocks)
    results = (coeffs, gram, ancestors[None])
    return pl.pallas_call(
        functools.partial(deliver, len(results)),
        out_shape=tuple(jax.ShapeDtypeStruct(x.shape, x.dtype) for x in results),
        in_specs=[hbm] * len(results),
        out_specs=(hbm,) * len(results),
        scratch_shapes=[pltpu.VMEM(x.shape, x.dtype) for x in results] + [dma((2, len(results)))],
        compiler_params=pltpu.CompilerParams(vmem_limit_bytes=62 * 1024 * 1024),
    )(*results)


def solution(mesh):
    return jax.shard_map(
        functools.partial(shards, mesh.shape["leaf"], mesh.shape["samp"]),
        mesh=mesh,
        in_specs=(
            P("leaf", "samp"),
            P("leaf", "samp"),
            P("leaf", None, None),
            P("leaf", None, None, None),
            P("leaf", None),
            P("leaf"),
            P("leaf", None),
            P(),
        ),
        out_specs=(P("leaf", None, "samp"), P("leaf", "samp"), P("leaf", None, None, "samp")),
        check_vma=False,
    )
```

```python
import functools

import jax
import jax.numpy as jnp
from jax import lax
from jax.experimental import pallas as pl
from jax.experimental.pallas import tpu as pltpu
from jax.sharding import PartitionSpec as P

MESH = pl.DeviceIdType.MESH
F32 = jnp.float32
BF16 = jnp.bfloat16


def split(x):
    high = x.astype(BF16)
    return high, (x - high.astype(F32)).astype(BF16)


def dot_nt(a, b):
    return lax.dot_general(a, b, (((1,), (1,)), ((), ())), preferred_element_type=F32)


def dot(a, b):
    return jnp.dot(a, b, preferred_element_type=F32)


def chain_step(rows, mats):
    high, low = split(rows)
    n = rows.shape[0]
    both = dot_nt(jnp.concatenate([high, low], axis=0), mats)
    return both[:n] + both[n:]


def kernel(
    n_leaf, n_samp, total_columns,
    index_ref, count_ref, inner_hbm, upper_hbm, omega_hbm, samples_hbm, basis_hbm, near_hbm,
    coeff_hbm, gram_hbm, ancestor_ref,
    inner_ref, upper_ref, omega_v, samples_v, basis_v, near_v, land_l, land_r, held,
    inner_v, upper_v, paths, ascend, leaf_path, up_acc, up_send, up_recv,
    gram_send, gram_recv, gram_sum, gram_mix, gram_ref, coeff_v, far_v,
    load_sem, near_sem, send_l, send_r, recv_l, recv_r,
    gram_ssem, gram_rsem, up_ssem, up_rsem, out_sem,
):
    leaf = lax.axis_index("leaf")
    samp = lax.axis_index("samp")
    leaf_count, rank, leaf_size = basis_v.shape
    slots = near_v.shape[1]
    width = omega_v.shape[0]
    pairs = leaf_count // 2
    half = pairs // 2
    heights = ancestor_ref.shape[0]
    steps = half
    part = rank // n_samp
    nodes = inner_ref.shape[0]

    load_omega = pltpu.make_async_copy(omega_hbm, omega_v, load_sem.at[0])
    load_samples = pltpu.make_async_copy(samples_hbm, samples_v, load_sem.at[1])
    load_basis = pltpu.make_async_copy(basis_hbm, basis_v, load_sem.at[2])
    load_near = pltpu.make_async_copy(near_hbm, near_v, near_sem)
    load_inner = pltpu.make_async_copy(inner_hbm, inner_ref, load_sem.at[3])
    load_upper = pltpu.make_async_copy(upper_hbm, upper_ref, load_sem.at[4])
    load_inner.start()
    load_upper.start()
    load_omega.start()
    load_samples.start()
    load_basis.start()
    load_near.start()

    barrier = pltpu.get_barrier_semaphore()
    for d in range(1, n_leaf):
        pl.semaphore_signal(barrier, inc=1, device_id=(leaf ^ d, samp), device_id_type=MESH)
    for d in range(1, n_samp):
        pl.semaphore_signal(barrier, inc=1, device_id=(leaf, samp ^ d), device_id_type=MESH)

    pl.semaphore_wait(barrier, n_leaf + n_samp - 2)

    def lanes(pair):
        unit = 2 * leaf_size
        return pl.ds(pl.multiple_of(pair * unit, unit), unit)

    def to_right(c):
        at = lanes(pairs - 1 - c)
        return pltpu.make_async_remote_copy(
            src_ref=omega_hbm.at[:, at], dst_ref=land_l.at[:, at],
            send_sem=send_r.at[c], recv_sem=recv_l.at[c],
            device_id=(leaf + 1, samp), device_id_type=MESH,
        )

    def to_left(c):
        at = lanes(c)
        return pltpu.make_async_remote_copy(
            src_ref=omega_hbm.at[:, at], dst_ref=land_r.at[:, at],
            send_sem=send_l.at[c], recv_sem=recv_r.at[c],
            device_id=(leaf - 1, samp), device_id_type=MESH,
        )

    def send(c):
        @pl.when(leaf < n_leaf - 1)
        def _():
            to_right(c).start()

        @pl.when(leaf > 0)
        def _():
            to_left(c).start()

    window = 4

    def pump(c):
        @pl.when(leaf < n_leaf - 1)
        def _():
            to_right(c).wait_send()

        @pl.when(leaf > 0)
        def _():
            to_left(c).wait_send()

        @pl.when(c + window < pairs)
        def _():
            send(c + window)

    for c in range(window):
        send(c)

    load_inner.wait()
    load_upper.wait()
    lines = rank * rank // 128
    for r in range(lines):
        if r == lines // 2:
            pump(0)
        for src, dst in ((inner_ref, inner_v), (upper_ref, upper_v)):
            count = src.shape[0]
            tile = src[:, 128 * r:128 * r + 128].astype(F32)
            dst[pl.ds(2 * r, count, stride=rank), :] = tile
            dst[pl.ds(2 * r + 1, count, stride=rank), :] = pltpu.roll(tile, 64, 1)

    pump(1)

    eye = (
        lax.broadcasted_iota(jnp.int32, (rank, rank), 0)
        == lax.broadcasted_iota(jnp.int32, (rank, rank), 1)
    ).astype(F32)
    rows = None
    starts = []
    offset = 0
    for h in range(heights):
        starts.append(offset)
        offset += n_leaf >> h
    for h in reversed(range(heights)):
        node = starts[h] + lax.shift_right_logical(leaf, h)
        mat = upper_v[pl.ds(pl.multiple_of(node * rank, rank), rank), :][:, :rank].astype(BF16)
        rows = eye if rows is None else jnp.concatenate([eye, rows], axis=0)
        rows = chain_step(rows, mat)
    rows_high, rows_low = split(rows)
    ascend[...] = jnp.concatenate([rows_high, rows_high, rows_low], axis=1)
    paths[nodes] = eye

    pumped = 2
    for q in reversed(range(leaf_count - 1)):
        mats = inner_v[q * 2 * rank:(q + 1) * 2 * rank, :]
        both = chain_step(paths[leaf_count + q], mats[:, :rank].astype(BF16))
        if q < pairs:
            high, low = split(both)
            leaf_path[q] = jnp.concatenate([high, high, low], axis=1)
        else:
            paths[2 * q] = both[:, :rank]
            paths[2 * q + 1] = pltpu.roll(both, 64, 1)[:, :rank]
        if q % 4 == 0 and pumped <= half:
            pump(pumped)
            pumped += 1
    for c in range(pumped, half + 1):
        pump(c)

    def accept(src, at_held, lo):
        both = src[:, lanes(lo)]
        held[at_held + 2 * lo] = both[:, :leaf_size]
        held[at_held + 2 * lo + 1] = both[:, leaf_size:]

    load_omega.wait()
    for i in range(pairs):
        accept(omega_v, leaf_count, i)
    up_acc[...] = jnp.zeros_like(up_acc)
    load_samples.wait()
    load_basis.wait()
    load_near.wait()

    lower = lax.broadcasted_iota(jnp.int32, (leaf_size, 128), 1) < 64
    base = leaf * leaf_count - leaf_count

    def near_product(p):
        tiles = []
        for k in range(slots):
            at = jnp.clip(index_ref[k, p] - base, 0, 3 * leaf_count - 1)
            live = jnp.where(k < count_ref[p], 1.0, 0.0)
            tiles.append(held[at] * jnp.full((1, leaf_size), live, F32).astype(BF16))
        blocks = jnp.concatenate([near_v[p, k] for k in range(slots)], axis=1)
        return dot_nt(jnp.concatenate(tiles, axis=1), blocks)

    def near_stage(u, w):
        near = jnp.concatenate([near_product(2 * u), near_product(2 * u + 1)], axis=0)
        mine = samples_v[:, lanes(u)]
        mine = jnp.concatenate([mine[:, :leaf_size], mine[:, leaf_size:]], axis=0)
        far_v[w] = (mine.astype(F32) - near).astype(BF16)

    def post_stage(u, w):
        far = far_v[w]
        basis = basis_v[pl.ds(2 * u, 2)].reshape(2 * rank, leaf_size)
        both = dot_nt(basis, far)
        top, bottom = both[:rank], both[rank:]
        coeff_v[2 * u] = top[:, :width]
        coeff_v[2 * u + 1] = pltpu.roll(bottom, 64, 1)[:, :width]
        low_lane = lower[:rank]
        top = jnp.where(low_lane, top, 0.0)
        bottom = jnp.where(low_lane, 0.0, bottom)
        top_high, top_low = split(top)
        bottom_high, bottom_low = split(bottom)
        block_high = jnp.concatenate([top_high, bottom_high], axis=0)
        block_low = jnp.concatenate([top_low, bottom_low], axis=0)
        row_high = top_high + bottom_high
        row_low = top_low + bottom_low
        gram = dot_nt(
            jnp.concatenate([row_high, row_high, row_low], axis=1),
            jnp.concatenate([block_high, block_low, block_high], axis=1),
        ) * (1.0 / total_columns)
        for t in range(n_samp):
            gram_send[t, pl.ds(pl.multiple_of(w * part, part), part), :] = (
                gram[t * part:(t + 1) * part].astype(gram_send.dtype)
            )
        return dot(leaf_path[u], jnp.concatenate([block_high, block_low, block_high], axis=0))

    def receive(c):
        @pl.when(leaf > 0)
        def _():
            to_right(c).wait_recv()
            accept(land_l, 0, pairs - 1 - c)

        @pl.when(leaf < n_leaf - 1)
        def _():
            to_left(c).wait_recv()
            accept(land_r, 2 * leaf_count, c)

    for c in range(half):
        receive(c)

    span = 4 * part

    def gram_copy(d, j):
        at = pl.ds(pl.multiple_of(j * span, span), span)
        return pltpu.make_async_remote_copy(
            src_ref=gram_send.at[samp ^ d, at], dst_ref=gram_recv.at[d - 1, at],
            send_sem=gram_ssem.at[d - 1, j], recv_sem=gram_rsem.at[d - 1, j],
            device_id=(leaf, samp ^ d), device_id_type=MESH,
        )

    quarter = leaf_count // 4

    def out_copy(i):
        at = pl.ds((quarter, 0, 3 * quarter)[i], (2 * quarter, quarter, quarter)[i])
        return pltpu.make_async_copy(coeff_v.at[at], coeff_hbm.at[at], out_sem.at[i])

    def nears(j):
        near_stage(half - 1 - j, 2 * j)
        near_stage(half + j, 2 * j + 1)

    def posts(j):
        up_acc[...] += post_stage(half - 1 - j, 2 * j) + post_stage(half + j, 2 * j + 1)

    receive(half)
    nears(0)
    pump(half + 1)

    def step(j, carry):
        receive(half + j)
        posts(j - 1)
        nears(j)

        @pl.when(j % 2 == 0)
        def _():
            for d in range(1, n_samp):
                gram_copy(d, j // 2 - 1).start()

        @pl.when(j < steps - 1)
        def _():
            pump(half + 1 + j)

        @pl.when(j == steps // 2)
        def _():
            out_copy(0).start()

        return carry

    lax.fori_loop(1, steps, step, 0)
    posts(steps - 1)
    for d in range(1, n_samp):
        gram_copy(d, steps // 2 - 1).start()

    total = up_acc[...]
    total_high, total_low = split(total + pltpu.roll(total, 64, 1))
    total = dot(ascend[...], jnp.concatenate([total_high, total_low, total_high], axis=0))
    side = rank // 2
    shares = []
    for h in range(heights):
        share = jnp.where(
            lower[:side], total[h * rank:h * rank + side], total[h * rank + side:(h + 1) * rank]
        )
        up_send[h * side:(h + 1) * side] = share.astype(BF16)
        shares.append(share)

    def up_copy(d):
        first = (d.bit_length() - 1) * side
        at = pl.ds(first, heights * side - first)
        return pltpu.make_async_remote_copy(
            src_ref=up_send.at[at], dst_ref=up_recv.at[d - 1, at],
            send_sem=up_ssem.at[d - 1], recv_sem=up_rsem.at[d - 1],
            device_id=(leaf ^ d, samp), device_id_type=MESH,
        )

    for d in range(1, n_leaf):
        up_copy(d).start()
    out_copy(1).start()
    out_copy(2).start()

    def gram_wait(j, carry):
        for d in range(1, n_samp):
            gram_copy(d, j).wait_recv()
        return carry

    lax.fori_loop(0, steps // 2, gram_wait, 0)
    for w in range(pairs):
        u = half - 1 - w // 2 if w % 2 == 0 else half + w // 2
        at = slice(w * part, (w + 1) * part)
        value = gram_send[samp, at, :].astype(F32)
        for d in range(1, n_samp):
            value = value + gram_recv[d - 1, at, :].astype(F32)
        gram_sum[u * part:(u + 1) * part, :] = value
    low16 = lower[:pairs]
    for m in range(part // 2):
        first = gram_sum[pl.ds(2 * m, pairs, stride=part), :]
        second = gram_sum[pl.ds(2 * m + 1, pairs, stride=part), :]
        even = jnp.where(low16, first, pltpu.roll(second, 64, 1))
        odd = jnp.where(low16, pltpu.roll(first, 64, 1), second)
        lo = m * leaf_count
        gram_mix[pl.ds(lo, pairs, stride=2), :] = even
        gram_mix[pl.ds(lo + 1, pairs, stride=2), :] = odd
        gram_ref[:, 128 * m:128 * m + 128] = gram_mix[lo:lo + leaf_count, :]

    gram_out = pltpu.make_async_copy(gram_ref, gram_hbm, out_sem.at[3])
    gram_out.start()
    for d in range(1, n_leaf):
        up_copy(d).wait_recv()
    for h in range(heights):
        at = slice(h * side, (h + 1) * side)
        value = shares[h]
        for d in range(1, n_leaf):
            if d.bit_length() <= h + 1:
                value = value + up_recv[d - 1, at, :].astype(F32)
        ancestor_ref[h, 0:side, :] = value[:, :width]
        ancestor_ref[h, side:rank, :] = pltpu.roll(value, 64, 1)[:, :width]

    def finish(j, carry):
        for d in range(1, n_samp):
            gram_copy(d, j).wait_send()
        return carry

    lax.fori_loop(0, steps // 2, finish, 0)

    gram_out.wait()
    for i in range(3):
        out_copy(i).wait()
    for d in range(1, n_leaf):
        up_copy(d).wait_send()


def deliver(count, *refs):
    sources, targets, rooms = refs[:count], refs[count:2 * count], refs[2 * count:3 * count]
    sems = refs[-1]
    reads = [pltpu.make_async_copy(sources[i], rooms[i], sems.at[0, i]) for i in range(count)]
    writes = [pltpu.make_async_copy(rooms[i], targets[i], sems.at[1, i]) for i in range(count)]
    for read in reads:
        read.start()
    for read, write in zip(reads, writes):
        read.wait()
        write.start()
    for write in writes:
        write.wait()


def shards(
    n_leaf, n_samp,
    samples, omega, leaf_basis, near_blocks, near_index, near_count, inner_transfer, upper_transfer
):
    leaf_count, rank, leaf_size = leaf_basis.shape
    width = samples.shape[1]
    pairs = leaf_count // 2
    steps = pairs // 2
    heights = n_leaf.bit_length() - 1
    part = rank // n_samp
    nodes = inner_transfer.shape[0]
    upper_nodes = upper_transfer.shape[0]
    wire = BF16 if part % 16 == 0 else F32
    omega, samples, near_index = omega.T, samples.T, near_index.T
    vmem = pl.BlockSpec(memory_space=pltpu.VMEM)
    smem = pl.BlockSpec(memory_space=pltpu.SMEM)
    hbm = pl.BlockSpec(memory_space=pl.ANY)
    dma = pltpu.SemaphoreType.DMA
    coeffs, gram, ancestors = pl.pallas_call(
        functools.partial(kernel, n_leaf, n_samp, width * n_samp),
        out_shape=(
            jax.ShapeDtypeStruct((leaf_count, rank, width), F32),
            jax.ShapeDtypeStruct((leaf_count, part * rank), F32),
            jax.ShapeDtypeStruct((heights, rank, width), F32),
        ),
        in_specs=[smem, smem, hbm, hbm, hbm, hbm, hbm, hbm],
        out_specs=(hbm, hbm, vmem),
        scratch_shapes=[
            pltpu.VMEM(inner_transfer.shape, BF16),
            pltpu.VMEM(upper_transfer.shape, BF16),
            pltpu.VMEM(omega.shape, BF16),
            pltpu.VMEM(samples.shape, BF16),
            pltpu.VMEM(leaf_basis.shape, BF16),
            pltpu.VMEM(near_blocks.shape, BF16),
            pltpu.VMEM(omega.shape, BF16),
            pltpu.VMEM(omega.shape, BF16),
            pltpu.VMEM((3 * leaf_count, width, leaf_size), BF16),
            pltpu.VMEM((nodes * rank, 128), F32),
            pltpu.VMEM((upper_nodes * rank, 128), F32),
            pltpu.VMEM((nodes + 1, rank, rank), F32),
            pltpu.VMEM((heights * rank, 3 * rank), BF16),
            pltpu.VMEM((pairs, rank, 384), BF16),
            pltpu.VMEM((rank, 128), F32),
            pltpu.VMEM((heights * rank // 2, 128), BF16),
            pltpu.VMEM((n_leaf - 1, heights * rank // 2, 128), BF16),
            pltpu.VMEM((n_samp, pairs * part, 128), wire),
            pltpu.VMEM((n_samp - 1, pairs * part, 128), wire),
            pltpu.VMEM((pairs * part, 128), F32),
            pltpu.VMEM((part // 2 * leaf_count, 128), F32),
            pltpu.VMEM((leaf_count, part * rank), F32),
            pltpu.VMEM((leaf_count, rank, width), F32),
            pltpu.VMEM((pairs, leaf_size, leaf_size), BF16),
            dma((5,)), dma,
            dma((pairs,)), dma((pairs,)), dma((pairs,)), dma((pairs,)),
            dma((n_samp - 1, steps // 2)), dma((n_samp - 1, steps // 2)),
            dma((n_leaf - 1,)), dma((n_leaf - 1,)),
            dma((4,)),
        ],
        compiler_params=pltpu.CompilerParams(
            collective_id=0, has_side_effects=True, vmem_limit_bytes=56 * 1024 * 1024
        ),
    )(near_index, near_count, inner_transfer, upper_transfer, omega, samples, leaf_basis, near_blocks)
    results = (coeffs, gram, ancestors[None])
    return pl.pallas_call(
        functools.partial(deliver, len(results)),
        out_shape=tuple(jax.ShapeDtypeStruct(x.shape, x.dtype) for x in results),
        in_specs=[hbm] * len(results),
        out_specs=(hbm,) * len(results),
        scratch_shapes=[pltpu.VMEM(x.shape, x.dtype) for x in results] + [dma((2, len(results)))],
        compiler_params=pltpu.CompilerParams(vmem_limit_bytes=62 * 1024 * 1024),
    )(*results)


def solution(mesh):
    return jax.shard_map(
        functools.partial(shards, mesh.shape["leaf"], mesh.shape["samp"]),
        mesh=mesh,
        in_specs=(
            P("leaf", "samp"),
            P("leaf", "samp"),
            P("leaf", None, None),
            P("leaf", None, None, None),
            P("leaf", None),
            P("leaf"),
            P("leaf", None),
            P(),
        ),
        out_specs=(P("leaf", None, "samp"), P("leaf", "samp"), P("leaf", None, None, "samp")),
        check_vma=False,
    )
```

```python
import functools

import jax
import jax.numpy as jnp
from jax import lax
from jax.experimental import pallas as pl
from jax.experimental.pallas import tpu as pltpu
from jax.sharding import PartitionSpec as P

MESH = pl.DeviceIdType.MESH
F32 = jnp.float32
BF16 = jnp.bfloat16


def split(x):
    high = x.astype(BF16)
    return high, (x - high.astype(F32)).astype(BF16)


def dot_nt(a, b):
    return lax.dot_general(a, b, (((1,), (1,)), ((), ())), preferred_element_type=F32)


def dot(a, b):
    return jnp.dot(a, b, preferred_element_type=F32)


def chain_step(rows, mats):
    high, low = split(rows)
    n = rows.shape[0]
    both = dot_nt(jnp.concatenate([high, low], axis=0), mats)
    return both[:n] + both[n:]


def kernel(
    n_leaf, n_samp, total_columns,
    index_ref, count_ref, inner_hbm, upper_hbm, omega_hbm, samples_hbm, basis_hbm, near_hbm,
    coeff_hbm, gram_hbm, ancestor_ref,
    inner_ref, upper_ref, omega_v, samples_v, basis_v, near_v, land_l, land_r, held,
    inner_v, upper_v, paths, ascend, leaf_path, up_acc, up_send, up_recv,
    gram_send, gram_recv, gram_sum, gram_mix, gram_ref, coeff_v, far_v,
    load_sem, near_sem, send_l, send_r, recv_l, recv_r,
    gram_ssem, gram_rsem, up_ssem, up_rsem, out_sem,
):
    leaf = lax.axis_index("leaf")
    samp = lax.axis_index("samp")
    leaf_count, rank, leaf_size = basis_v.shape
    slots = near_v.shape[1]
    width = omega_v.shape[0]
    pairs = leaf_count // 2
    half = pairs // 2
    heights = ancestor_ref.shape[0]
    steps = half
    part = rank // n_samp
    nodes = inner_ref.shape[0]

    load_omega = pltpu.make_async_copy(omega_hbm, omega_v, load_sem.at[0])
    load_samples = pltpu.make_async_copy(samples_hbm, samples_v, load_sem.at[1])
    load_basis = pltpu.make_async_copy(basis_hbm, basis_v, load_sem.at[2])
    load_near = pltpu.make_async_copy(near_hbm, near_v, near_sem)
    load_inner = pltpu.make_async_copy(inner_hbm, inner_ref, load_sem.at[3])
    load_upper = pltpu.make_async_copy(upper_hbm, upper_ref, load_sem.at[4])
    load_inner.start()
    load_upper.start()
    load_omega.start()
    load_samples.start()
    load_basis.start()
    load_near.start()

    barrier = pltpu.get_barrier_semaphore()
    for d in range(1, n_leaf):
        pl.semaphore_signal(barrier, inc=1, device_id=(leaf ^ d, samp), device_id_type=MESH)
    for d in range(1, n_samp):
        pl.semaphore_signal(barrier, inc=1, device_id=(leaf, samp ^ d), device_id_type=MESH)

    pl.semaphore_wait(barrier, n_leaf + n_samp - 2)

    def lanes(pair):
        unit = 2 * leaf_size
        return pl.ds(pl.multiple_of(pair * unit, unit), unit)

    def to_right(c):
        at = lanes(pairs - 1 - c)
        return pltpu.make_async_remote_copy(
            src_ref=omega_hbm.at[:, at], dst_ref=land_l.at[:, at],
            send_sem=send_r.at[c], recv_sem=recv_l.at[c],
            device_id=(leaf + 1, samp), device_id_type=MESH,
        )

    def to_left(c):
        at = lanes(c)
        return pltpu.make_async_remote_copy(
            src_ref=omega_hbm.at[:, at], dst_ref=land_r.at[:, at],
            send_sem=send_l.at[c], recv_sem=recv_r.at[c],
            device_id=(leaf - 1, samp), device_id_type=MESH,
        )

    def send(c):
        @pl.when(leaf < n_leaf - 1)
        def _():
            to_right(c).start()

        @pl.when(leaf > 0)
        def _():
            to_left(c).start()

    window = 4

    def pump(c):
        @pl.when(leaf < n_leaf - 1)
        def _():
            to_right(c).wait_send()

        @pl.when(leaf > 0)
        def _():
            to_left(c).wait_send()

        @pl.when(c + window < pairs)
        def _():
            send(c + window)

    for c in range(window):
        send(c)

    load_inner.wait()
    load_upper.wait()
    lines = rank * rank // 128
    for r in range(lines):
        if r == lines // 2:
            pump(0)
        for src, dst in ((inner_ref, inner_v), (upper_ref, upper_v)):
            count = src.shape[0]
            tile = src[:, 128 * r:128 * r + 128].astype(F32)
            dst[pl.ds(2 * r, count, stride=rank), :] = tile
            dst[pl.ds(2 * r + 1, count, stride=rank), :] = pltpu.roll(tile, 64, 1)

    pump(1)

    eye = (
        lax.broadcasted_iota(jnp.int32, (rank, rank), 0)
        == lax.broadcasted_iota(jnp.int32, (rank, rank), 1)
    ).astype(F32)
    rows = None
    starts = []
    offset = 0
    for h in range(heights):
        starts.append(offset)
        offset += n_leaf >> h
    for h in reversed(range(heights)):
        node = starts[h] + lax.shift_right_logical(leaf, h)
        mat = upper_v[pl.ds(pl.multiple_of(node * rank, rank), rank), :][:, :rank].astype(BF16)
        rows = eye if rows is None else jnp.concatenate([eye, rows], axis=0)
        rows = chain_step(rows, mat)
    rows_high, rows_low = split(rows)
    ascend[...] = jnp.concatenate([rows_high, rows_high, rows_low], axis=1)
    paths[nodes] = eye

    pumped = 2
    for q in reversed(range(leaf_count - 1)):
        mats = inner_v[q * 2 * rank:(q + 1) * 2 * rank, :]
        both = chain_step(paths[leaf_count + q], mats[:, :rank].astype(BF16))
        if q < pairs:
            high, low = split(both)
            leaf_path[q] = jnp.concatenate([high, high, low], axis=1)
        else:
            paths[2 * q] = both[:, :rank]
            paths[2 * q + 1] = pltpu.roll(both, 64, 1)[:, :rank]
        if q % 4 == 0 and pumped <= half:
            pump(pumped)
            pumped += 1
    for c in range(pumped, half + 1):
        pump(c)

    def accept(src, at_held, lo):
        both = src[:, lanes(lo)]
        held[at_held + 2 * lo] = both[:, :leaf_size]
        held[at_held + 2 * lo + 1] = both[:, leaf_size:]

    load_omega.wait()
    for i in range(pairs):
        accept(omega_v, leaf_count, i)
    up_acc[...] = jnp.zeros_like(up_acc)
    load_samples.wait()
    load_basis.wait()
    load_near.wait()

    lower = lax.broadcasted_iota(jnp.int32, (leaf_size, 128), 1) < 64
    base = leaf * leaf_count - leaf_count

    def near_product(p):
        tiles = []
        for k in range(slots):
            at = jnp.clip(index_ref[k, p] - base, 0, 3 * leaf_count - 1)
            live = jnp.where(k < count_ref[p], 1.0, 0.0)
            tiles.append(held[at] * jnp.full((1, leaf_size), live, F32).astype(BF16))
        blocks = jnp.concatenate([near_v[p, k] for k in range(slots)], axis=1)
        return dot_nt(jnp.concatenate(tiles, axis=1), blocks)

    def near_stage(u, w):
        near = jnp.concatenate([near_product(2 * u), near_product(2 * u + 1)], axis=0)
        mine = samples_v[:, lanes(u)]
        mine = jnp.concatenate([mine[:, :leaf_size], mine[:, leaf_size:]], axis=0)
        far_v[w] = (mine.astype(F32) - near).astype(BF16)

    def post_stage(u, w):
        far = far_v[w]
        basis = basis_v[pl.ds(2 * u, 2)].reshape(2 * rank, leaf_size)
        both = dot_nt(basis, far)
        top, bottom = both[:rank], both[rank:]
        coeff_v[2 * u] = top[:, :width]
        coeff_v[2 * u + 1] = pltpu.roll(bottom, 64, 1)[:, :width]
        low_lane = lower[:rank]
        top = jnp.where(low_lane, top, 0.0)
        bottom = jnp.where(low_lane, 0.0, bottom)
        top_high, top_low = split(top)
        bottom_high, bottom_low = split(bottom)
        block_high = jnp.concatenate([top_high, bottom_high], axis=0)
        block_low = jnp.concatenate([top_low, bottom_low], axis=0)
        row_high = top_high + bottom_high
        row_low = top_low + bottom_low
        gram = dot_nt(
            jnp.concatenate([row_high, row_high, row_low], axis=1),
            jnp.concatenate([block_high, block_low, block_high], axis=1),
        ) * (1.0 / total_columns)
        for t in range(n_samp):
            gram_send[t, pl.ds(pl.multiple_of(w * part, part), part), :] = (
                gram[t * part:(t + 1) * part].astype(gram_send.dtype)
            )
        return dot(leaf_path[u], jnp.concatenate([block_high, block_low, block_high], axis=0))

    def receive(c):
        @pl.when(leaf > 0)
        def _():
            to_right(c).wait_recv()
            accept(land_l, 0, pairs - 1 - c)

        @pl.when(leaf < n_leaf - 1)
        def _():
            to_left(c).wait_recv()
            accept(land_r, 2 * leaf_count, c)

    for c in range(half):
        receive(c)

    span = 4 * part

    def gram_copy(d, j):
        at = pl.ds(pl.multiple_of(j * span, span), span)
        return pltpu.make_async_remote_copy(
            src_ref=gram_send.at[samp ^ d, at], dst_ref=gram_recv.at[d - 1, at],
            send_sem=gram_ssem.at[d - 1, j], recv_sem=gram_rsem.at[d - 1, j],
            device_id=(leaf, samp ^ d), device_id_type=MESH,
        )

    quarter = leaf_count // 4

    def out_copy(i):
        at = pl.ds((quarter, 0, 3 * quarter)[i], (2 * quarter, quarter, quarter)[i])
        return pltpu.make_async_copy(coeff_v.at[at], coeff_hbm.at[at], out_sem.at[i])

    def nears(j):
        near_stage(half - 1 - j, 2 * j)
        near_stage(half + j, 2 * j + 1)

    def posts(j):
        up_acc[...] += post_stage(half - 1 - j, 2 * j) + post_stage(half + j, 2 * j + 1)

    receive(half)
    nears(0)
    pump(half + 1)

    def step(j, carry):
        receive(half + j)
        posts(j - 1)
        nears(j)

        @pl.when(j % 2 == 0)
        def _():
            for d in range(1, n_samp):
                gram_copy(d, j // 2 - 1).start()

        pump(half + 1 + j)

        @pl.when(j == steps // 2)
        def _():
            out_copy(0).start()

        return carry

    lax.fori_loop(1, steps - 1, step, 0)
    posts(steps - 2)
    receive(pairs - 1)
    nears(steps - 1)
    posts(steps - 1)

    total = up_acc[...]
    total_high, total_low = split(total + pltpu.roll(total, 64, 1))
    total = dot(ascend[...], jnp.concatenate([total_high, total_low, total_high], axis=0))
    side = rank // 2
    shares = []
    for h in range(heights):
        share = jnp.where(
            lower[:side], total[h * rank:h * rank + side], total[h * rank + side:(h + 1) * rank]
        )
        up_send[h * side:(h + 1) * side] = share.astype(BF16)
        shares.append(share)

    def up_copy(d):
        first = (d.bit_length() - 1) * side
        at = pl.ds(first, heights * side - first)
        return pltpu.make_async_remote_copy(
            src_ref=up_send.at[at], dst_ref=up_recv.at[d - 1, at],
            send_sem=up_ssem.at[d - 1], recv_sem=up_rsem.at[d - 1],
            device_id=(leaf ^ d, samp), device_id_type=MESH,
        )

    for d in reversed(range(1, n_leaf)):
        up_copy(d).start()
    for d in range(1, n_samp):
        gram_copy(d, steps // 2 - 1).start()
    out_copy(1).start()
    out_copy(2).start()

    def gram_wait(j, carry):
        for d in range(1, n_samp):
            gram_copy(d, j).wait_recv()
        return carry

    lax.fori_loop(0, steps // 2, gram_wait, 0)
    for w in range(pairs):
        u = half - 1 - w // 2 if w % 2 == 0 else half + w // 2
        at = slice(w * part, (w + 1) * part)
        value = gram_send[samp, at, :].astype(F32)
        for d in range(1, n_samp):
            value = value + gram_recv[d - 1, at, :].astype(F32)
        gram_sum[u * part:(u + 1) * part, :] = value
    low16 = lower[:pairs]
    for m in range(part // 2):
        first = gram_sum[pl.ds(2 * m, pairs, stride=part), :]
        second = gram_sum[pl.ds(2 * m + 1, pairs, stride=part), :]
        even = jnp.where(low16, first, pltpu.roll(second, 64, 1))
        odd = jnp.where(low16, pltpu.roll(first, 64, 1), second)
        lo = m * leaf_count
        gram_mix[pl.ds(lo, pairs, stride=2), :] = even
        gram_mix[pl.ds(lo + 1, pairs, stride=2), :] = odd
        gram_ref[:, 128 * m:128 * m + 128] = gram_mix[lo:lo + leaf_count, :]

    gram_out = pltpu.make_async_copy(gram_ref, gram_hbm, out_sem.at[3])
    gram_out.start()
    for d in range(1, n_leaf):
        up_copy(d).wait_recv()
    for h in range(heights):
        at = slice(h * side, (h + 1) * side)
        value = shares[h]
        for d in range(1, n_leaf):
            if d.bit_length() <= h + 1:
                value = value + up_recv[d - 1, at, :].astype(F32)
        ancestor_ref[h, 0:side, :] = value[:, :width]
        ancestor_ref[h, side:rank, :] = pltpu.roll(value, 64, 1)[:, :width]

    def finish(j, carry):
        for d in range(1, n_samp):
            gram_copy(d, j).wait_send()
        return carry

    lax.fori_loop(0, steps // 2, finish, 0)

    gram_out.wait()
    for i in range(3):
        out_copy(i).wait()
    for d in range(1, n_leaf):
        up_copy(d).wait_send()


def deliver(count, *refs):
    sources, targets, rooms = refs[:count], refs[count:2 * count], refs[2 * count:3 * count]
    sems = refs[-1]
    reads = [pltpu.make_async_copy(sources[i], rooms[i], sems.at[0, i]) for i in range(count)]
    writes = [pltpu.make_async_copy(rooms[i], targets[i], sems.at[1, i]) for i in range(count)]
    for read in reads:
        read.start()
    for read, write in zip(reads, writes):
        read.wait()
        write.start()
    for write in writes:
        write.wait()


def shards(
    n_leaf, n_samp,
    samples, omega, leaf_basis, near_blocks, near_index, near_count, inner_transfer, upper_transfer
):
    leaf_count, rank, leaf_size = leaf_basis.shape
    width = samples.shape[1]
    pairs = leaf_count // 2
    steps = pairs // 2
    heights = n_leaf.bit_length() - 1
    part = rank // n_samp
    nodes = inner_transfer.shape[0]
    upper_nodes = upper_transfer.shape[0]
    wire = BF16 if part % 16 == 0 else F32
    omega, samples, near_index = omega.T, samples.T, near_index.T
    vmem = pl.BlockSpec(memory_space=pltpu.VMEM)
    smem = pl.BlockSpec(memory_space=pltpu.SMEM)
    hbm = pl.BlockSpec(memory_space=pl.ANY)
    dma = pltpu.SemaphoreType.DMA
    coeffs, gram, ancestors = pl.pallas_call(
        functools.partial(kernel, n_leaf, n_samp, width * n_samp),
        out_shape=(
            jax.ShapeDtypeStruct((leaf_count, rank, width), F32),
            jax.ShapeDtypeStruct((leaf_count, part * rank), F32),
            jax.ShapeDtypeStruct((heights, rank, width), F32),
        ),
        in_specs=[smem, smem, hbm, hbm, hbm, hbm, hbm, hbm],
        out_specs=(hbm, hbm, vmem),
        scratch_shapes=[
            pltpu.VMEM(inner_transfer.shape, BF16),
            pltpu.VMEM(upper_transfer.shape, BF16),
            pltpu.VMEM(omega.shape, BF16),
            pltpu.VMEM(samples.shape, BF16),
            pltpu.VMEM(leaf_basis.shape, BF16),
            pltpu.VMEM(near_blocks.shape, BF16),
            pltpu.VMEM(omega.shape, BF16),
            pltpu.VMEM(omega.shape, BF16),
            pltpu.VMEM((3 * leaf_count, width, leaf_size), BF16),
            pltpu.VMEM((nodes * rank, 128), F32),
            pltpu.VMEM((upper_nodes * rank, 128), F32),
            pltpu.VMEM((nodes + 1, rank, rank), F32),
            pltpu.VMEM((heights * rank, 3 * rank), BF16),
            pltpu.VMEM((pairs, rank, 384), BF16),
            pltpu.VMEM((rank, 128), F32),
            pltpu.VMEM((heights * rank // 2, 128), BF16),
            pltpu.VMEM((n_leaf - 1, heights * rank // 2, 128), BF16),
            pltpu.VMEM((n_samp, pairs * part, 128), wire),
            pltpu.VMEM((n_samp - 1, pairs * part, 128), wire),
            pltpu.VMEM((pairs * part, 128), F32),
            pltpu.VMEM((part // 2 * leaf_count, 128), F32),
            pltpu.VMEM((leaf_count, part * rank), F32),
            pltpu.VMEM((leaf_count, rank, width), F32),
            pltpu.VMEM((pairs, leaf_size, leaf_size), BF16),
            dma((5,)), dma,
            dma((pairs,)), dma((pairs,)), dma((pairs,)), dma((pairs,)),
            dma((n_samp - 1, steps // 2)), dma((n_samp - 1, steps // 2)),
            dma((n_leaf - 1,)), dma((n_leaf - 1,)),
            dma((4,)),
        ],
        compiler_params=pltpu.CompilerParams(
            collective_id=0, has_side_effects=True, vmem_limit_bytes=56 * 1024 * 1024
        ),
    )(near_index, near_count, inner_transfer, upper_transfer, omega, samples, leaf_basis, near_blocks)
    results = (coeffs, gram, ancestors[None])
    return pl.pallas_call(
        functools.partial(deliver, len(results)),
        out_shape=tuple(jax.ShapeDtypeStruct(x.shape, x.dtype) for x in results),
        in_specs=[hbm] * len(results),
        out_specs=(hbm,) * len(results),
        scratch_shapes=[pltpu.VMEM(x.shape, x.dtype) for x in results] + [dma((2, len(results)))],
        compiler_params=pltpu.CompilerParams(vmem_limit_bytes=62 * 1024 * 1024),
    )(*results)


def solution(mesh):
    return jax.shard_map(
        functools.partial(shards, mesh.shape["leaf"], mesh.shape["samp"]),
        mesh=mesh,
        in_specs=(
            P("leaf", "samp"),
            P("leaf", "samp"),
            P("leaf", None, None),
            P("leaf", None, None, None),
            P("leaf", None),
            P("leaf"),
            P("leaf", None),
            P(),
        ),
        out_specs=(P("leaf", None, "samp"), P("leaf", "samp"), P("leaf", None, None, "samp")),
        check_vma=False,
    )
```
